512 devices in a mesh: span: 16 (over y, core), cross: 32 (over x, z).
Axes of the slice: x: 4, y: 8, z: 8, core: 2. Of those that a mesh axis runs over, the one named last changes fastest.
Arguments:
- right_side: float32 [512, 1024, 128], P('span', 'cross')
- shift: float32 [512, 1024, 128], P('span', 'cross'), may hold values from 0.05 to 2
- tile_mask: int32 [16, 32], P('span', 'cross'), may hold values from 0 to 1, as said below
- owner_lists: int32 [16, 32, 12], P('span', 'cross'), may hold values from 0 to 32, as said below
- owner_ids: int32 [16, 32], P('span', 'cross'), may hold values from 0 to 31, as said below
Outputs:
- pressure: float32 [512, 1024, 128], P('span', 'cross')
- residual: float32 [512, 1024, 128], P('span', 'cross')
The draws below stay inside these ranges and needn't reach their ends.
Inputs may be any that keep to these rules, and one draw needn't show every extreme that they name: `tile_mask`: 24 tiles of each span row are 1. `owner_lists`: each span row has 4 owners, themselves masked tiles; every masked tile stands in exactly one list, that of owner_ids, in increasing order of a drawn rank; lists of non-owners are all 32, lists are padded at the end with 32; in every span row one owner's list is full. `owner_ids`: on unmasked tiles the tile's own cross index.
All inputs are finite; a program needn't handle non-finite values.
Results may differ from the reference program's by a relative error of at most 0.000051.
Values sent between devices are 32-bit elements; how exact they have to be, the bound alone decides.
No kernel may reach another device: no remote copies, remote signals or barrier semaphores. Data moves between devices by JAX's collectives and lax.ppermute only.
A program may use at most 64 MiB of HBM per device.

```python
import math
import jax
import jax.numpy as jnp

COLUMN_CELLS = 128
LEVELS = 4
SWEEPS = 4
COARSE_SWEEPS = 4
COARSE_SPAN = 2
COARSE_CROSS = 2
COARSE_COLUMN = 8
MASKED = 24
OWNERS = 4
OWNER_SLOTS = 12
GRID_SPAN = 512
GRID_CROSS = 1024
N_SPAN = 16
N_CROSS = 32


def assign_row(row_key):
    order_key, extra_key = jax.random.split(row_key)
    order = jax.random.permutation(order_key, N_CROSS).astype(jnp.int32)
    positions = jnp.arange(N_CROSS, dtype=jnp.int32)
    extra = 1 + jax.random.randint(extra_key, (N_CROSS,), 0, OWNERS - 1).astype(jnp.int32)
    group = jnp.where(positions < OWNER_SLOTS, 0, jnp.where(positions < MASKED, extra, OWNERS))
    ranks = jnp.argsort(order).astype(jnp.int32)
    masked = (ranks < MASKED).astype(jnp.int32)
    tile_group = jnp.clip(group[ranks], 0, OWNERS - 1)
    owner_of_tile = jnp.where(masked == 1, order[tile_group], positions)
    owner_range = jnp.arange(OWNERS, dtype=jnp.int32)
    scores = jnp.where(group[None, :] == owner_range[:, None], positions[None, :], N_CROSS + positions[None, :])
    firsts = jnp.sort(scores, axis=1)[:, :OWNER_SLOTS]
    entries = jnp.where(firsts < N_CROSS, order[firsts % N_CROSS], N_CROSS)
    lists = jnp.where((ranks < OWNERS)[:, None], entries[jnp.clip(ranks, 0, OWNERS - 1)], N_CROSS)
    return (masked, owner_of_tile.astype(jnp.int32), lists.astype(jnp.int32))


def assign_tiles(key):
    row_keys = jax.random.split(key, N_SPAN)
    return jax.vmap(assign_row)(row_keys)


def draw_tile_mask(key, part):
    masked, owner_of_tile, lists = assign_tiles(key)
    return masked


def draw_owner_lists(key, part):
    masked, owner_of_tile, lists = assign_tiles(key)
    return lists


def draw_owner_ids(key, part):
    masked, owner_of_tile, lists = assign_tiles(key)
    return owner_of_tile


def draw_right_side(key, part):
    key = jax.random.fold_in(key, 7)
    shape = (GRID_SPAN, GRID_CROSS, COLUMN_CELLS)
    return jax.random.normal(key, shape, jnp.float32)


def level_of(key, shape, pieces, smallest, largest):
    def one(axis_at, parts):
        heights = jax.random.uniform(jax.random.fold_in(jax.random.fold_in(key, 6), axis_at), (parts,), jnp.float32, smallest / len(pieces), largest / len(pieces))
        return jnp.repeat(jnp.exp(heights), shape[axis_at] // parts).reshape((-1,) + (1,) * (len(shape) - axis_at - 1))

    gain = one(*pieces[0])
    for cut in pieces[1:]:
        gain = gain * one(*cut)
    return gain


def setup_inputs(seed: int = 0) -> dict:
    arg_keys = jax.random.split(jax.random.key(seed), 6)
    return {
        "right_side": draw_right_side(jax.random.fold_in(arg_keys[5], 71), 0),
        "shift": jnp.clip(jnp.exp(math.log(2.0) - 3.6888794 * jax.random.uniform(arg_keys[1], (GRID_SPAN, GRID_CROSS, COLUMN_CELLS), jnp.float32) ** level_of(arg_keys[1], (GRID_SPAN, GRID_CROSS, COLUMN_CELLS), ((0, 16), (1, 32)), -0.2, 0.2)), 0.05, 2.0),
        "tile_mask": draw_tile_mask(jax.random.fold_in(arg_keys[5], 71), 0),
        "owner_lists": draw_owner_lists(jax.random.fold_in(arg_keys[5], 71), 0),
        "owner_ids": draw_owner_ids(jax.random.fold_in(arg_keys[5], 71), 0),
    }


DAMPING = 0.8


def neighbours(values):
    padded = jnp.pad(values, 1)
    beside = padded[2:, 1:-1, 1:-1] + padded[:-2, 1:-1, 1:-1]
    beside = beside + padded[1:-1, 2:, 1:-1] + padded[1:-1, :-2, 1:-1]
    beside = beside + padded[1:-1, 1:-1, 2:] + padded[1:-1, 1:-1, :-2]
    return beside


def apply_operator(values, shift):
    return (6.0 + shift) * values - neighbours(values)


def sweep(values, right_side, shift):
    return values + DAMPING * (right_side - apply_operator(values, shift)) / (6.0 + shift)


def strip_sweeps(strips):
    widths = [(0, 0)] * (strips.ndim - 3) + [(1, 1)] * 3
    solution = jnp.zeros_like(strips)
    for sweep_index in range(COARSE_SWEEPS):
        padded = jnp.pad(solution, widths)
        beside = padded[..., 2:, 1:-1, 1:-1] + padded[..., :-2, 1:-1, 1:-1]
        beside = beside + padded[..., 1:-1, 2:, 1:-1] + padded[..., 1:-1, :-2, 1:-1]
        beside = beside + padded[..., 1:-1, 1:-1, 2:] + padded[..., 1:-1, 1:-1, :-2]
        solution = solution + DAMPING * (strips - (6.0 * solution - beside)) / 6.0
    return solution


def reference(right_side, shift, tile_mask, owner_lists, owner_ids):
    factor = 2 ** LEVELS
    pressure = jnp.zeros_like(right_side)
    for sweep_index in range(SWEEPS):
        pressure = sweep(pressure, right_side, shift)
    fine_residual = right_side - apply_operator(pressure, shift)
    shaped = fine_residual.reshape(N_SPAN, COARSE_SPAN, factor, N_CROSS, COARSE_CROSS, factor, COARSE_COLUMN, factor)
    coarse = jnp.sum(shaped, axis=(2, 5, 7)) / float(factor)
    coarse = jnp.transpose(coarse, (0, 2, 1, 3, 4))
    flat_blocks = coarse.reshape(N_SPAN, N_CROSS, -1)
    positions = jnp.arange(N_CROSS, dtype=jnp.int32)
    chosen = jnp.sum((owner_lists[..., None] == positions).astype(jnp.float32), axis=2)
    strips = chosen[..., None] * flat_blocks[:, None, :, :]
    strips = strips.reshape(N_SPAN, N_CROSS, N_CROSS, COARSE_SPAN, COARSE_CROSS, COARSE_COLUMN)
    strips = jnp.transpose(strips, (0, 1, 3, 2, 4, 5))
    strips = strips.reshape(N_SPAN, N_CROSS, COARSE_SPAN, N_CROSS * COARSE_CROSS, COARSE_COLUMN)
    solution = strip_sweeps(strips)
    solution = solution.reshape(N_SPAN, N_CROSS, COARSE_SPAN, N_CROSS, COARSE_CROSS, COARSE_COLUMN)
    solution = jnp.transpose(solution, (0, 1, 3, 2, 4, 5)).reshape(N_SPAN, N_CROSS, N_CROSS, -1)
    per_position = jnp.transpose(solution, (0, 2, 1, 3))
    one_hot = (owner_ids[..., None] == positions).astype(jnp.float32)
    tile_solution = jnp.sum(one_hot[..., None] * per_position, axis=2)
    tile_solution = tile_solution.reshape(coarse.shape)
    correction = tile_solution * tile_mask.astype(jnp.float32)[:, :, None, None, None]
    correction = jnp.transpose(correction, (0, 2, 1, 3, 4))
    expanded = jnp.broadcast_to(correction[:, :, None, :, :, None, :, None], shaped.shape)
    pressure = pressure + expanded.reshape(right_side.shape)
    for sweep_index in range(SWEEPS):
        pressure = sweep(pressure, right_side, shift)
    residual = right_side - apply_operator(pressure, shift)
    return pressure, residual
```

```python
import functools

import jax
import jax.numpy as jnp
from jax import lax
from jax.experimental import pallas as pl
from jax.experimental.pallas import tpu as pltpu
from jax.sharding import PartitionSpec as P

DAMPING = 0.8
N = 32
LANES = 128
WIDE = N + 16
HALO = 4
REACH = 5
ROWS_W = N + 2 * HALO
ROWS_V = N + 2 * REACH
CUBE = 16
F32 = jnp.float32


def iota(shape, axis):
    return lax.broadcasted_iota(jnp.int32, shape, axis)


def neighbours(prev, cur, nxt):
    cells = cur.shape[0]
    lane = iota(cur.shape, 1)
    low = jnp.where(lane == 0, 0.0, pltpu.roll(cur, 1, 1))
    high = jnp.where(lane == LANES - 1, 0.0, pltpu.roll(cur, LANES - 1, 1))
    beside = pltpu.roll(cur, 1, 0) + pltpu.roll(cur, cells - 1, 0)
    return (prev + nxt) + beside + (low + high)


def sweep_rows(v_ref, w_ref, wb_ref, low, high):
    def body(r, carry):
        prev, cur = carry
        nxt = v_ref[r + 1]
        beside = neighbours(prev, cur, nxt)
        v_ref[r] = (1.0 - DAMPING) * cur + (wb_ref[r - 1] + w_ref[r - 1] * beside)
        return cur, nxt

    lax.fori_loop(low, high, body, (v_ref[low - 1], v_ref[low]), unroll=2)


def prepare_kernel(b_ref, s_ref, w_ref, wb_ref, down_ref, up_ref):
    for r in range(N):
        w = DAMPING / (6.0 + s_ref[r])
        wb = w * b_ref[r]
        w_ref[r] = w
        wb_ref[r] = wb
        if r < HALO:
            up_ref[0, r] = w
            up_ref[1, r] = wb
        if r >= N - HALO:
            down_ref[0, r - (N - HALO)] = w
            down_ref[1, r - (N - HALO)] = wb


def edges_kernel(w_ref, wb_ref, above_ref, below_ref, right_ref, left_ref):
    sub = iota((8, LANES), 0)
    for r in range(ROWS_W):
        if r < HALO:
            w, wb = above_ref.at[0, r], above_ref.at[1, r]
        elif r < HALO + N:
            w, wb = w_ref.at[r - HALO], wb_ref.at[r - HALO]
        else:
            w, wb = below_ref.at[0, r - HALO - N], below_ref.at[1, r - HALO - N]
        right_ref[r] = jnp.where(sub < 4, pltpu.roll(w[N - 8 : N], 4, 0), wb[N - 8 : N])
        left_ref[r] = jnp.where(sub < 4, w[0:8], pltpu.roll(wb[0:8], 4, 0))


def first_kernel(
    b_ref, s_ref, w_ref, wb_ref, above_ref, below_ref, from_left_ref, from_right_ref, mask_ref, id_ref,
    v_ref, ww_ref, wwb_ref, down_ref, up_ref, coarse_ref,
):
    span, cross = lax.axis_index("span"), lax.axis_index("cross")
    has_up, has_down = span > 0, span < lax.axis_size("span") - 1
    has_left, has_right = cross > 0, cross < lax.axis_size("cross") - 1
    sub = iota((8, LANES), 0)
    for r in range(ROWS_W):
        if r < HALO:
            w, wb = above_ref[0, r], above_ref[1, r]
        elif r < HALO + N:
            w, wb = w_ref[r - HALO], wb_ref[r - HALO]
        else:
            w, wb = below_ref[0, r - HALO - N], below_ref[1, r - HALO - N]
        in_left = (sub >= 4) & has_left
        in_right = (sub < 4) & has_right
        if r < HALO or r >= HALO + N:
            inside = has_up if r < HALO else has_down
            w, wb = jnp.where(inside, w, 0.0), jnp.where(inside, wb, 0.0)
            in_left, in_right = in_left & inside, in_right & inside
        left, right = from_left_ref[r], from_right_ref[r]
        wb_left = jnp.where(in_left, left, 0.0)
        wb_right = jnp.where(in_right, pltpu.roll(right, 4, 0), 0.0)
        ww_ref[r, 0:8] = jnp.where(in_left, pltpu.roll(left, 4, 0), 0.0)
        ww_ref[r, 8 : 8 + N] = w
        ww_ref[r, 8 + N :] = jnp.where(in_right, right, 0.0)
        wwb_ref[r, 0:8] = wb_left
        wwb_ref[r, 8 : 8 + N] = wb
        wwb_ref[r, 8 + N :] = wb_right
        v_ref[r + 1, 0:8] = wb_left
        v_ref[r + 1, 8 : 8 + N] = wb
        v_ref[r + 1, 8 + N :] = wb_right
    for step in range(1, 4):
        sweep_rows(v_ref, ww_ref, wwb_ref, 1 + step, ROWS_V - 1 - step)

    rows = []
    for part in range(2):
        start = REACH + part * CUBE

        def body(r, carry):
            prev, cur, total = carry
            nxt = v_ref[r + 1]
            beside = neighbours(prev, cur, nxt)[8 : 8 + N]
            own = cur[8 : 8 + N]
            fine = b_ref[r - REACH] - ((6.0 + s_ref[r - REACH]) * own - beside)
            return cur, nxt, total + fine

        zero = jnp.zeros((N, LANES), F32)
        _, _, total = lax.fori_loop(start, start + CUBE, body, (v_ref[start - 1], v_ref[start], zero), unroll=2)
        for half in range(2):
            rows.append(jnp.sum(total[half * CUBE : (half + 1) * CUBE], axis=0, keepdims=True))
    tile = jnp.zeros((8, LANES), F32)
    for i, row in enumerate(rows):
        tile = jnp.where(sub == i, row, tile)
    lane = iota((8, LANES), 1)
    for step in (1, 2, 4, 8):
        tile = tile + jnp.where((lane & step) == 0, pltpu.roll(tile, LANES - step, 1), pltpu.roll(tile, step, 1))
    tile = tile / float(CUBE)
    tile = jnp.where(sub == 4, id_ref[0, 0].astype(F32), tile)
    tile = jnp.where(sub == 5, mask_ref[0, 0].astype(F32), tile)
    coarse_ref[...] = tile
    for k in range(4):
        for q in range(4):
            down_ref[4 * k + q] = v_ref[REACH + N - 5 + k, 8 + 8 * q : 16 + 8 * q]
            up_ref[4 * k + q] = v_ref[REACH + 1 + k, 8 + 8 * q : 16 + 8 * q]
    down_ref[16] = tile
    up_ref[16] = tile


def second_edges_kernel(v_ref, above_ref, below_ref, coarse_ref, right_ref, left_ref, far_ref):
    sub = iota((8, LANES), 0)
    for k in range(17):
        a, c = REACH - 1 + k, REACH - 1 + 17 + k
        right_ref[k] = jnp.where((sub >= 3) & (sub < 7), v_ref[a, N : N + 8], pltpu.roll(v_ref[c, N : N + 8], 4, 0))
        left_ref[k] = jnp.where((sub >= 1) & (sub < 5), v_ref[a, 8:16], pltpu.roll(v_ref[c, 8:16], 4, 0))
    for k in range(3):
        right_ref[17 + k] = above_ref[4 * (k + 1) + 3]
        left_ref[17 + k] = above_ref[4 * (k + 1)]
        right_ref[20 + k] = below_ref[4 * k + 3]
        left_ref[20 + k] = below_ref[4 * k]
    for k, source in enumerate((above_ref.at[16], coarse_ref, below_ref.at[16])):
        right_ref[23 + k] = source[...]
        left_ref[23 + k] = source[...]
        far_ref[k] = source[...]


def second_kernel(
    b_ref, s_ref, v_in_ref, ww_ref, wwb_ref, above_ref, below_ref, coarse_ref, from_left_ref, from_right_ref,
    far_left_ref, far_right_ref, pressure_ref, residual_ref, v_ref, e_ref,
):
    span, cross = lax.axis_index("span"), lax.axis_index("cross")
    n_cross = lax.axis_size("cross")
    has_up, has_down = span > 0, span < lax.axis_size("span") - 1
    has_left, has_right = cross > 0, cross < n_cross - 1
    sub = iota((8, LANES), 0)
    lane = iota((8, LANES), 1)
    even = (sub & 1) == 0

    def wide(row):
        return jnp.broadcast_to(row, (8, LANES))

    scale = [
        jnp.where((cross + d >= 0) & (cross + d < n_cross), F32(DAMPING / 6.0), F32(0.0)) for d in range(-2, 3)
    ]
    middle = (above_ref.at[16], coarse_ref, below_ref.at[16])
    for rho in range(3):
        tiles = (
            far_left_ref.at[rho], from_left_ref.at[23 + rho], middle[rho], from_right_ref.at[23 + rho],
            far_right_ref.at[rho],
        )
        ids = [wide(t[4:5]) for t in tiles]
        masks = [wide(t[5:6]) for t in tiles]
        owner = jnp.where(sub < 2, ids[1], jnp.where(sub < 4, ids[2], ids[3]))
        strip = []
        for d in range(5):
            chosen = (ids[d] == owner) & (masks[d] > 0.5)
            for j in range(2):
                cells = jnp.where(even, wide(tiles[d][j : j + 1]), wide(tiles[d][2 + j : 3 + j]))
                strip.append(jnp.where(chosen, cells, 0.0))
        e = [scale[j // 2] * strip[j] for j in range(10)]
        for step in range(1, 4):
            new = list(e)
            for j in range(step, 10 - step):
                beside = e[j - 1] + e[j + 1]
                beside = beside + jnp.where(even, pltpu.roll(e[j], 7, 0), pltpu.roll(e[j], 1, 0))
                beside = beside + jnp.where(lane < CUBE, 0.0, pltpu.roll(e[j], CUBE, 1))
                beside = beside + jnp.where(lane >= LANES - CUBE, 0.0, pltpu.roll(e[j], LANES - CUBE, 1))
                new[j] = (1.0 - DAMPING) * e[j] + scale[j // 2] * (strip[j] + beside)
            e = new
        mask = jnp.where(
            sub < 2, jnp.where(has_left, masks[1], 0.0), jnp.where(sub < 4, masks[2], jnp.where(has_right, masks[3], 0.0))
        )
        if rho != 1:
            mask = jnp.where(has_up if rho == 0 else has_down, mask, 0.0)
        for j in range(3, 7):
            e_ref[rho, j - 3] = e[j] * mask

    def correction(rho, j, side, i):
        k = 2 * side + i
        return wide(e_ref[rho, j - 3, k : k + 1])

    def own(rho, i):
        first, second = correction(rho, 4, 1, i), correction(rho, 5, 1, i)
        return jnp.concatenate([first, first, second, second], axis=0)

    zero = jnp.zeros((8, LANES), F32)
    for r in range(ROWS_V):
        cell = r - REACH
        rho = 0 if cell < 0 else (1 if cell < N else 2)
        i = 1 if cell < 0 else (cell // CUBE if cell < N else 0)
        inside = (has_up, None, has_down)[rho]
        if cell < -1 or cell > N:
            source, k = (above_ref, cell + 5) if cell < 0 else (below_ref, cell - N - 1)
            for q in range(4):
                v_ref[r, 8 + 8 * q : 16 + 8 * q] = jnp.where(inside, source[4 * k + q], 0.0) + correction(
                    rho, 4 + q // 2, 1, i
                )
            if cell == -REACH or cell == N + REACH - 1:
                left, right = zero, zero
            else:
                k = 17 + cell + 4 if cell < 0 else 20 + cell - N - 1
                left = jnp.where(inside & has_left, from_left_ref[k], 0.0)
                right = jnp.where(inside & has_right, from_right_ref[k], 0.0)
        else:
            v_ref[r, 8 : 8 + N] = v_in_ref[r, 8 : 8 + N] + own(rho, i)
            k = cell + 1
            left, right = from_left_ref[k % 17], from_right_ref[k % 17]
            if k >= 17:
                left, right = pltpu.roll(left, 4, 0), pltpu.roll(right, 4, 0)
            in_left, in_right = has_left, has_right
            if rho != 1:
                in_left, in_right = in_left & inside, in_right & inside
            left = jnp.where((sub >= 3) & (sub < 7) & in_left, left, jnp.where(sub == 7, v_in_ref[r, 0:8], 0.0))
            right = jnp.where((sub >= 1) & (sub < 5) & in_right, right, jnp.where(sub == 0, v_in_ref[r, 8 + N :], 0.0))
        v_ref[r, 0:8] = left + correction(rho, 3, 0, i)
        v_ref[r, 8 + N :] = right + correction(rho, 6, 2, i)

    for step in range(4):
        sweep_rows(v_ref, ww_ref, wwb_ref, 1 + step, ROWS_V - 1 - step)

    def body(r, carry):
        prev, cur = carry
        nxt = v_ref[r + 1]
        beside = neighbours(prev, cur, nxt)[8 : 8 + N]
        mine = cur[8 : 8 + N]
        pressure_ref[r - REACH] = mine
        residual_ref[r - REACH] = b_ref[r - REACH] - ((6.0 + s_ref[r - REACH]) * mine - beside)
        return cur, nxt

    lax.fori_loop(REACH, REACH + N, body, (v_ref[REACH - 1], v_ref[REACH]), unroll=2)


def call(kernel, outs, args, scalars=0, scratch=()):
    vmem = pl.BlockSpec(memory_space=pltpu.VMEM)
    smem = pl.BlockSpec(memory_space=pltpu.SMEM)
    return pl.pallas_call(
        kernel,
        out_shape=[jax.ShapeDtypeStruct(s, F32) for s in outs],
        in_specs=[vmem] * (len(args) - scalars) + [smem] * scalars,
        out_specs=[vmem] * len(outs),
        scratch_shapes=[pltpu.VMEM(s, F32) for s in scratch],
        compiler_params=pltpu.CompilerParams(vmem_limit_bytes=32 * 1024 * 1024),
    )(*args)


def shifted(block, axis, step):
    count = lax.axis_size(axis)
    return lax.ppermute(block, axis, [(i, (i + step) % count) for i in range(count)])


def on_device(right_side, shift, tile_mask, owner_lists, owner_ids):
    block = (N, N, LANES)
    w, wb, down, up = call(
        prepare_kernel, [block, block, (2, HALO, N, LANES), (2, HALO, N, LANES)], [right_side, shift]
    )
    above = shifted(down, "span", 1)
    below = shifted(up, "span", -1)
    right, left = call(edges_kernel, [(ROWS_W, 8, LANES)] * 2, [w, wb, above, below])
    from_left = shifted(right, "cross", 1)
    from_right = shifted(left, "cross", -1)
    v, ww, wwb, down, up, coarse = call(
        first_kernel,
        [
            (ROWS_V, WIDE, LANES), (ROWS_W, WIDE, LANES), (ROWS_W, WIDE, LANES), (17, 8, LANES), (17, 8, LANES),
            (8, LANES),
        ],
        [right_side, shift, w, wb, above, below, from_left, from_right, tile_mask, owner_ids],
        scalars=2,
    )
    above = shifted(down, "span", 1)
    below = shifted(up, "span", -1)
    right, left, far = call(
        second_edges_kernel, [(26, 8, LANES), (26, 8, LANES), (3, 8, LANES)], [v, above, below, coarse]
    )
    from_left = shifted(right, "cross", 1)
    from_right = shifted(left, "cross", -1)
    far_left = shifted(far, "cross", 2)
    far_right = shifted(far, "cross", -2)
    pressure, residual = call(
        second_kernel,
        [block, block],
        [right_side, shift, v, ww, wwb, above, below, coarse, from_left, from_right, far_left, far_right],
        scratch=[(ROWS_V, WIDE, LANES), (3, 4, 8, LANES)],
    )
    return (pressure, residual)


def solution(mesh):
    return jax.shard_map(
        on_device,
        mesh=mesh,
        in_specs=(
            P("span", "cross", None),
            P("span", "cross", None),
            P("span", "cross"),
            P("span", "cross", None),
            P("span", "cross"),
        ),
        out_specs=(P("span", "cross", None), P("span", "cross", None)),
        check_vma=False,
    )
```

```python
import math

import jax
import jax.numpy as jnp
from jax import lax
from jax.experimental import pallas as pl
from jax.experimental.pallas import tpu as pltpu
from jax.sharding import PartitionSpec as P

DAMPING = 0.8
N = 32
LANES = 128
WIDE = N + 16
HALO = 4
REACH = 5
ROWS_W = N + 2 * HALO
ROWS_V = N + 2 * REACH
CUBE = 16
F32 = jnp.float32


def iota(shape, axis):
    return lax.broadcasted_iota(jnp.int32, shape, axis)


def neighbours(prev, cur, nxt):
    cells = cur.shape[0]
    lane = iota(cur.shape, 1)
    low = jnp.where(lane == 0, 0.0, pltpu.roll(cur, 1, 1))
    high = jnp.where(lane == LANES - 1, 0.0, pltpu.roll(cur, LANES - 1, 1))
    beside = pltpu.roll(cur, 1, 0) + pltpu.roll(cur, cells - 1, 0)
    return (prev + nxt) + beside + (low + high)


def sweeps(v_ref, w_ref, wb_ref, low, high, count):
    def one(step, carry):
        prev, cur = v_ref[low - 1], v_ref[low]
        for r in range(low, high):
            nxt = v_ref[r + 1]
            beside = neighbours(prev, cur, nxt)
            v_ref[r] = (1.0 - DAMPING) * cur + (wb_ref[r - 1] + w_ref[r - 1] * beside)
            prev, cur = cur, nxt
        return carry

    lax.fori_loop(0, count, one, 0)


def edges_kernel(b_ref, s_ref, right_ref, left_ref, b_left, b_right, s_left, s_right, sems):
    copies = [
        pltpu.make_async_copy(source.at[:, pl.ds(start, 8), :], target, sems.at[n])
        for n, (source, start, target) in enumerate(
            ((s_ref, N - 8, s_right), (b_ref, N - 8, b_right), (s_ref, 0, s_left), (b_ref, 0, b_left))
        )
    ]
    for copy in copies:
        copy.start()
    sub = iota((8, LANES), 0)
    copies[0].wait()
    copies[1].wait()
    for r in range(N):
        w = DAMPING / (6.0 + s_right[r])
        right_ref[r] = jnp.where(sub < 4, pltpu.roll(w, 4, 0), w * b_right[r])
    copies[2].wait()
    copies[3].wait()
    for r in range(N):
        w = DAMPING / (6.0 + s_left[r])
        left_ref[r] = jnp.where(sub < 4, w, pltpu.roll(w * b_left[r], 4, 0))


def coefficients_kernel(b_ref, s_ref, mask_ref, id_ref, w_ref, wb_ref, info_ref):
    for r in range(N):
        w = DAMPING / (6.0 + s_ref[r])
        w_ref[r] = w
        wb_ref[r] = w * b_ref[r]
    sub = iota((8, LANES), 0)
    number = jnp.broadcast_to(id_ref[...].astype(F32), (8, LANES))
    mask = jnp.broadcast_to(mask_ref[...].astype(F32), (8, LANES))
    info_ref[...] = jnp.where(sub == 4, number, jnp.where(sub == 5, mask, 0.0))


def beside_of(left_msg, right_msg):
    sub = iota((8, LANES), 0)
    w = jnp.where(sub < 4, right_msg, pltpu.roll(left_msg, 4, 0))
    wb = jnp.where(sub < 4, pltpu.roll(right_msg, 4, 0), left_msg)
    return w, wb


def rows_kernel(w_ref, wb_ref, from_left_ref, from_right_ref, down_ref, up_ref):
    for target, start in ((up_ref, 0), (down_ref, N - HALO)):
        for k in range(HALO):
            r = start + k
            sides = beside_of(from_left_ref[r], from_right_ref[r])
            for a, ref in enumerate((w_ref, wb_ref)):
                target[a, k, 0:N] = ref[r]
                target[a, k, N:] = sides[a]


def first_kernel(
    b_ref, s_ref, w_ref, wb_ref, from_left_ref, from_right_ref, above_ref, below_ref, info_ref,
    v_ref, ww_ref, wwb_ref, right_ref, left_ref, coarse_ref,
):
    span, cross = lax.axis_index("span"), lax.axis_index("cross")
    has_up, has_down = span > 0, span < lax.axis_size("span") - 1
    has_left, has_right = cross > 0, cross < lax.axis_size("cross") - 1
    sub = iota((8, LANES), 0)
    for r in range(ROWS_W):
        in_left, in_right = (sub >= 4) & has_left, (sub < 4) & has_right
        if HALO <= r < HALO + N:
            w, wb = w_ref[r - HALO], wb_ref[r - HALO]
            w_side, wb_side = beside_of(from_left_ref[r - HALO], from_right_ref[r - HALO])
        else:
            source, k, inside = (above_ref, r, has_up) if r < HALO else (below_ref, r - HALO - N, has_down)
            w, wb = jnp.where(inside, source[0, k, 0:N], 0.0), jnp.where(inside, source[1, k, 0:N], 0.0)
            w_side, wb_side = source[0, k, N:], source[1, k, N:]
            in_left, in_right = in_left & inside, in_right & inside
        wb_left, wb_right = jnp.where(in_left, wb_side, 0.0), jnp.where(in_right, wb_side, 0.0)
        ww_ref[r, 0:8] = jnp.where(in_left, w_side, 0.0)
        ww_ref[r, 8 : 8 + N] = w
        ww_ref[r, 8 + N :] = jnp.where(in_right, w_side, 0.0)
        wwb_ref[r, 0:8] = wb_left
        wwb_ref[r, 8 : 8 + N] = wb
        wwb_ref[r, 8 + N :] = wb_right
        v_ref[r + 1, 0:8] = wb_left
        v_ref[r + 1, 8 : 8 + N] = wb
        v_ref[r + 1, 8 + N :] = wb_right
    sweeps(v_ref, ww_ref, wwb_ref, 2, ROWS_V - 2, 3)

    tile = info_ref[...]
    prev, cur = v_ref[REACH - 1], v_ref[REACH]
    for part in range(2):
        total = None
        for r in range(part * CUBE, (part + 1) * CUBE):
            nxt = v_ref[r + REACH + 1]
            beside = neighbours(prev, cur, nxt)[8 : 8 + N]
            fine = b_ref[r] - ((6.0 + s_ref[r]) * cur[8 : 8 + N] - beside)
            total = fine if total is None else total + fine
            prev, cur = cur, nxt
        for half in range(2):
            row = jnp.sum(total[half * CUBE : (half + 1) * CUBE], axis=0, keepdims=True)
            tile = jnp.where(sub == 2 * part + half, row, tile)
    lane = iota((8, LANES), 1)
    cells = tile
    for step in (1, 2, 4, 8):
        cells = cells + jnp.where((lane & step) == 0, pltpu.roll(cells, LANES - step, 1), pltpu.roll(cells, step, 1))
    tile = jnp.where(sub < 4, cells / float(CUBE), tile)
    coarse_ref[...] = tile
    right_ref[16] = tile
    left_ref[16] = tile
    for k in range(16):
        a, c = REACH + k, REACH + 16 + k
        right_ref[k] = jnp.where((sub >= 3) & (sub < 7), v_ref[a, N : N + 8], pltpu.roll(v_ref[c, N : N + 8], 4, 0))
        left_ref[k] = jnp.where((sub >= 1) & (sub < 5), v_ref[a, 8:16], pltpu.roll(v_ref[c, 8:16], 4, 0))


def correct_kernel(
    v_in_ref, coarse_ref, far_left_ref, far_right_ref, from_left_ref, from_right_ref, v_ref, down_ref, up_ref, e_ref
):
    cross, n_cross = lax.axis_index("cross"), lax.axis_size("cross")
    has_left, has_right = cross > 0, cross < n_cross - 1
    sub = iota((8, LANES), 0)
    lane = iota((8, LANES), 1)
    even = (sub & 1) == 0

    def wide(row):
        return jnp.broadcast_to(row, (8, LANES))

    scale = [
        jnp.where((cross + d >= 0) & (cross + d < n_cross), F32(DAMPING / 6.0), F32(0.0)) for d in range(-2, 3)
    ]
    tiles = (far_left_ref, from_left_ref.at[16], coarse_ref, from_right_ref.at[16], far_right_ref)
    ids = [wide(t[4:5]) for t in tiles]
    masks = [wide(t[5:6]) for t in tiles]
    owner = jnp.where(sub < 2, ids[1], jnp.where(sub < 4, ids[2], ids[3]))
    strip = []
    for d in range(5):
        chosen = (ids[d] == owner) & (masks[d] > 0.5)
        for j in range(2):
            cells = jnp.where(even, wide(tiles[d][j : j + 1]), wide(tiles[d][2 + j : 3 + j]))
            strip.append(jnp.where(chosen, cells, 0.0))
    e = [scale[j // 2] * strip[j] for j in range(10)]
    for step in range(1, 4):
        new = list(e)
        for j in range(step, 10 - step):
            beside = e[j - 1] + e[j + 1]
            beside = beside + jnp.where(even, pltpu.roll(e[j], 7, 0), pltpu.roll(e[j], 1, 0))
            beside = beside + jnp.where(lane < CUBE, 0.0, pltpu.roll(e[j], CUBE, 1))
            beside = beside + jnp.where(lane >= LANES - CUBE, 0.0, pltpu.roll(e[j], LANES - CUBE, 1))
            new[j] = (1.0 - DAMPING) * e[j] + scale[j // 2] * (strip[j] + beside)
        e = new
    mask = jnp.where(
        sub < 2, jnp.where(has_left, masks[1], 0.0), jnp.where(sub < 4, masks[2], jnp.where(has_right, masks[3], 0.0))
    )
    for j in range(3, 7):
        e_ref[j - 3] = e[j] * mask

    in_left = (sub >= 3) & (sub < 7) & has_left
    in_right = (sub >= 1) & (sub < 5) & has_right
    for i in range(2):
        first, second = wide(e_ref[1, 2 + i : 3 + i]), wide(e_ref[2, 2 + i : 3 + i])
        own = jnp.concatenate([first, first, second, second], axis=0)
        beside = wide(e_ref[0, i : i + 1]), wide(e_ref[3, 4 + i : 5 + i])
        for k in range(CUBE):
            r = i * CUBE + k
            v_ref[r, 8 : 8 + N] = v_in_ref[r + REACH, 8 : 8 + N] + own
            left, right = from_left_ref[k], from_right_ref[k]
            if i == 1:
                left, right = pltpu.roll(left, 4, 0), pltpu.roll(right, 4, 0)
            left = jnp.where(in_left, left, jnp.where(sub == 7, v_in_ref[r + REACH, 0:8], 0.0))
            right = jnp.where(in_right, right, jnp.where(sub == 0, v_in_ref[r + REACH, 8 + N :], 0.0))
            v_ref[r, 0:8] = left + beside[0]
            v_ref[r, 8 + N :] = right + beside[1]
    for target, start in ((up_ref, 0), (down_ref, N - REACH)):
        for k in range(REACH):
            target[k, 0:N] = v_ref[start + k, 8 : 8 + N]
            target[k, N:] = jnp.where(sub < 4, v_ref[start + k, 8 + N :], v_ref[start + k, 0:8])


def second_kernel(
    b_ref, s_ref, v_in_ref, ww_ref, wwb_ref, above_ref, below_ref, pressure_ref, residual_ref, v_ref
):
    span = lax.axis_index("span")
    has_up, has_down = span > 0, span < lax.axis_size("span") - 1
    sub = iota((8, LANES), 0)
    for r in range(ROWS_V):
        if REACH <= r < REACH + N:
            v_ref[r] = v_in_ref[r - REACH]
        else:
            source, k, inside = (above_ref, r, has_up) if r < REACH else (below_ref, r - REACH - N, has_down)
            side = source[k, N:]
            v_ref[r, 0:8] = jnp.where((sub >= 4) & inside, side, 0.0)
            v_ref[r, 8 : 8 + N] = jnp.where(inside, source[k, 0:N], 0.0)
            v_ref[r, 8 + N :] = jnp.where((sub < 4) & inside, side, 0.0)
    sweeps(v_ref, ww_ref, wwb_ref, 1, ROWS_V - 1, 4)
    prev, cur = v_ref[REACH - 1], v_ref[REACH]
    for r in range(N):
        nxt = v_ref[r + REACH + 1]
        beside = neighbours(prev, cur, nxt)[8 : 8 + N]
        mine = cur[8 : 8 + N]
        pressure_ref[r] = mine
        residual_ref[r] = b_ref[r] - ((6.0 + s_ref[r]) * mine - beside)
        prev, cur = cur, nxt


def call(kernel, outs, args, scratch=(), spaces=None, ops=0, room=32):
    vmem = pl.BlockSpec(memory_space=pltpu.VMEM)
    size = 4 * sum(math.prod(s) for s in outs)
    return pl.pallas_call(
        kernel,
        out_shape=[jax.ShapeDtypeStruct(s, F32) for s in outs],
        in_specs=[spaces or vmem] * len(args),
        out_specs=[vmem] * len(outs),
        scratch_shapes=[pltpu.VMEM(s, F32) if isinstance(s, tuple) else s for s in scratch],
        compiler_params=pltpu.CompilerParams(vmem_limit_bytes=room * 1024 * 1024),
        cost_estimate=pl.CostEstimate(flops=ops, bytes_accessed=2 * size, transcendentals=0),
    )(*args)


def shifted(block, axis, step):
    count = lax.axis_size(axis)
    pairs = [(i, (i + step) % count) for i in range(count)]
    return lax.ppermute(block, axis, [p for p in pairs if axis == "span" or p[1] - p[0] == step])


def on_device(right_side, shift, tile_mask, owner_lists, owner_ids):
    block = (N, N, LANES)
    edge = (N, 8, LANES)
    right, left = call(
        edges_kernel,
        [edge, edge],
        [right_side, shift],
        scratch=[edge, edge, edge, edge, pltpu.SemaphoreType.DMA((4,))],
        spaces=pl.BlockSpec(memory_space=pltpu.HBM),
        room=62,
    )
    from_left = shifted(right, "cross", 1)
    from_right = shifted(left, "cross", -1)
    w, wb, info = call(coefficients_kernel, [block, block, (8, LANES)], [right_side, shift, tile_mask, owner_ids])
    rows = (2, HALO, N + 8, LANES)
    down, up = call(rows_kernel, [rows, rows], [w, wb, from_left, from_right])
    above = shifted(down, "span", 1)
    below = shifted(up, "span", -1)
    v, ww, wwb, right, left, coarse = call(
        first_kernel,
        [
            (ROWS_V, WIDE, LANES), (ROWS_W, WIDE, LANES), (ROWS_W, WIDE, LANES), (17, 8, LANES), (17, 8, LANES),
            (8, LANES),
        ],
        [right_side, shift, w, wb, from_left, from_right, above, below, info],
    )
    far_left = shifted(coarse, "cross", 2)
    far_right = shifted(coarse, "cross", -2)
    from_left = shifted(right, "cross", 1)
    from_right = shifted(left, "cross", -1)
    rows = (REACH, N + 8, LANES)
    v, down, up = call(
        correct_kernel,
        [(N, WIDE, LANES), rows, rows],
        [v, coarse, far_left, far_right, from_left, from_right],
        scratch=[(4, 8, LANES)],
    )
    above = shifted(down, "span", 1)
    below = shifted(up, "span", -1)
    pressure, residual = call(
        second_kernel,
        [block, block],
        [right_side, shift, v, ww, wwb, above, below],
        scratch=[(ROWS_V, WIDE, LANES)],
    )
    return (pressure, residual)


def solution(mesh):
    return jax.shard_map(
        on_device,
        mesh=mesh,
        in_specs=(
            P("span", "cross", None),
            P("span", "cross", None),
            P("span", "cross"),
            P("span", "cross", None),
            P("span", "cross"),
        ),
        out_specs=(P("span", "cross", None), P("span", "cross", None)),
        check_vma=False,
    )
```

```python
import math

import jax
import jax.numpy as jnp
from jax import lax
from jax.experimental import pallas as pl
from jax.experimental.pallas import tpu as pltpu
from jax.sharding import PartitionSpec as P

DAMPING = 0.8
N = 32
LANES = 128
WIDE = N + 16
HALO = 4
REACH = 5
ROWS_W = N + 2 * HALO
ROWS_V = N + 2 * REACH
CUBE = 16
F32 = jnp.float32


def iota(shape, axis):
    return lax.broadcasted_iota(jnp.int32, shape, axis)


def neighbours(prev, cur, nxt):
    cells = cur.shape[0]
    lane = iota(cur.shape, 1)
    low = jnp.where(lane == 0, 0.0, pltpu.roll(cur, 1, 1))
    high = jnp.where(lane == LANES - 1, 0.0, pltpu.roll(cur, LANES - 1, 1))
    beside = pltpu.roll(cur, 1, 0) + pltpu.roll(cur, cells - 1, 0)
    return (prev + nxt) + beside + (low + high)


def swept(prev, cur, nxt, w, wb):
    return (1.0 - DAMPING) * cur + (wb + w * neighbours(prev, cur, nxt))


def inner_sweeps(v_ref, w_ref, wb_ref, saved_ref, count):
    def one(step, carry):
        prev, cur = v_ref[0], v_ref[1]
        for r in range(1, N - 1):
            nxt = v_ref[r + 1]
            v_ref[r] = swept(prev, cur, nxt, w_ref[r], wb_ref[r])
            prev, cur = cur, nxt
        for k in range(2):
            saved_ref[0, step, k] = v_ref[step + 1 + k]
            saved_ref[1, step, k] = v_ref[N - 3 - step + k]
        return carry

    lax.fori_loop(0, count, one, 0)


def outer_sweeps(rows, first, count, side, coefficients, saved_ref):
    for step in range(count):
        new = [swept(*rows[i : i + 3], *coefficients(first + 1 + i)) for i in range(len(rows) - 2)]
        saved = [saved_ref[side, step, k] for k in range(2)]
        rows, first = (new + saved, first + 1) if side == 0 else (saved + new, first - 1)
    return rows, first


def fine_residual(prev, cur, nxt, b, s):
    own = slice(8, 8 + N)
    return b - ((6.0 + s) * cur[own] - neighbours(prev, cur, nxt)[own])


def edges_kernel(b_ref, s_ref, right_ref, left_ref, b_left, b_right, s_left, s_right, sems):
    copies = [
        pltpu.make_async_copy(source.at[:, pl.ds(start, 8), :], target, sems.at[n])
        for n, (source, start, target) in enumerate(
            ((s_ref, N - 8, s_right), (b_ref, N - 8, b_right), (s_ref, 0, s_left), (b_ref, 0, b_left))
        )
    ]
    for copy in copies:
        copy.start()
    sub = iota((8, LANES), 0)
    copies[0].wait()
    copies[1].wait()
    for r in range(N):
        w = DAMPING / (6.0 + s_right[r])
        right_ref[r] = jnp.where(sub < 4, pltpu.roll(w, 4, 0), w * b_right[r])
    copies[2].wait()
    copies[3].wait()
    for r in range(N):
        w = DAMPING / (6.0 + s_left[r])
        left_ref[r] = jnp.where(sub < 4, w, pltpu.roll(w * b_left[r], 4, 0))


def coefficients_kernel(b_ref, s_ref, mask_ref, id_ref, w_ref, wb_ref, info_ref):
    for r in range(N):
        w = DAMPING / (6.0 + s_ref[r])
        w_ref[r] = w
        wb_ref[r] = w * b_ref[r]
    sub = iota((8, LANES), 0)
    number = jnp.broadcast_to(id_ref[...].astype(F32), (8, LANES))
    mask = jnp.broadcast_to(mask_ref[...].astype(F32), (8, LANES))
    info_ref[...] = jnp.where(sub == 4, number, jnp.where(sub == 5, mask, 0.0))


def beside_of(left_msg, right_msg):
    sub = iota((8, LANES), 0)
    w = jnp.where(sub < 4, right_msg, pltpu.roll(left_msg, 4, 0))
    wb = jnp.where(sub < 4, pltpu.roll(right_msg, 4, 0), left_msg)
    return w, wb


def rows_kernel(w_ref, wb_ref, from_left_ref, from_right_ref, down_ref, up_ref):
    for target, start in ((up_ref, 0), (down_ref, N - HALO)):
        for k in range(HALO):
            r = start + k
            sides = beside_of(from_left_ref[r], from_right_ref[r])
            for a, ref in enumerate((w_ref, wb_ref)):
                target[a, k, 0:N] = ref[r]
                target[a, k, N:] = sides[a]


def first_inner_kernel(
    b_ref, s_ref, w_ref, wb_ref, from_left_ref, from_right_ref, v_ref, ww_ref, wwb_ref, saved_ref, partial_ref
):
    cross = lax.axis_index("cross")
    sub = iota((8, LANES), 0)
    in_left, in_right = (sub >= 4) & (cross > 0), (sub < 4) & (cross < lax.axis_size("cross") - 1)
    for r in range(N):
        w_side, wb_side = beside_of(from_left_ref[r], from_right_ref[r])
        for ref, own, side in ((ww_ref, w_ref[r], w_side), (wwb_ref, wb_ref[r], wb_side)):
            ref[r, 0:8] = jnp.where(in_left, side, 0.0)
            ref[r, 8 : 8 + N] = own
            ref[r, 8 + N :] = jnp.where(in_right, side, 0.0)
        v_ref[r] = wwb_ref[r]
    inner_sweeps(v_ref, ww_ref, wwb_ref, saved_ref, 3)
    for part in range(2):
        total = jnp.zeros((N, LANES), F32)
        for r in range(4 + 12 * part, 16 + 12 * part):
            total = total + fine_residual(v_ref[r - 1], v_ref[r], v_ref[r + 1], b_ref[r], s_ref[r])
        partial_ref[part] = total


def first_outer_kernel(
    b_ref, s_ref, v_ref, ww_ref, wwb_ref, saved_ref, partial_ref, above_ref, below_ref, info_ref,
    ends_ref, halo_ref, right_ref, left_ref, coarse_ref,
):
    span, cross = lax.axis_index("span"), lax.axis_index("cross")
    sub = iota((8, LANES), 0)
    in_left, in_right = (sub >= 4) & (cross > 0), (sub < 4) & (cross < lax.axis_size("cross") - 1)
    inside = (span > 0, span < lax.axis_size("span") - 1)
    for side, source in enumerate((above_ref, below_ref)):
        for a in range(2):
            for k in range(HALO):
                beside = source[a, k, N:]
                halo_ref[side, a, k, 0:8] = jnp.where(in_left & inside[side], beside, 0.0)
                halo_ref[side, a, k, 8 : 8 + N] = jnp.where(inside[side], source[a, k, 0:N], 0.0)
                halo_ref[side, a, k, 8 + N :] = jnp.where(in_right & inside[side], beside, 0.0)

    def coefficients(r):
        if 0 <= r < N:
            return ww_ref[r], wwb_ref[r]
        side, k = (0, r + HALO) if r < 0 else (1, r - N)
        return halo_ref[side, 0, k], halo_ref[side, 1, k]

    tile = info_ref[...]
    for side in range(2):
        start = -HALO if side == 0 else N - 2
        rows, start = outer_sweeps(
            [coefficients(r)[1] for r in range(start, start + HALO + 2)], start, 3, side, coefficients, saved_ref
        )
        total = partial_ref[side]
        for i in range(1, 5):
            r = start + i
            total = total + fine_residual(*rows[i - 1 : i + 2], b_ref[r], s_ref[r])
        for half in range(2):
            row = jnp.sum(total[half * CUBE : (half + 1) * CUBE], axis=0, keepdims=True)
            tile = jnp.where(sub == 2 * side + half, row, tile)
        for k in range(3):
            ends_ref[side, k] = rows[k + 1 + side]
    lane = iota((8, LANES), 1)
    cells = tile
    for step in (1, 2, 4, 8):
        cells = cells + jnp.where((lane & step) == 0, pltpu.roll(cells, LANES - step, 1), pltpu.roll(cells, step, 1))
    tile = jnp.where(sub < 4, cells / float(CUBE), tile)
    coarse_ref[...] = tile
    right_ref[16] = tile
    left_ref[16] = tile

    def pressure(r):
        return ends_ref.at[0, r] if r < 3 else (v_ref.at[r] if r < N - 3 else ends_ref.at[1, r - N + 3])

    for k in range(16):
        a, c = pressure(k), pressure(16 + k)
        right_ref[k] = jnp.where((sub >= 3) & (sub < 7), a[N : N + 8], pltpu.roll(c[N : N + 8], 4, 0))
        left_ref[k] = jnp.where((sub >= 1) & (sub < 5), a[8:16], pltpu.roll(c[8:16], 4, 0))


def correct_kernel(
    inner_ref, ends_ref, coarse_ref, far_left_ref, far_right_ref, from_left_ref, from_right_ref, v_ref, down_ref, up_ref, e_ref
):
    cross, n_cross = lax.axis_index("cross"), lax.axis_size("cross")
    has_left, has_right = cross > 0, cross < n_cross - 1
    sub = iota((8, LANES), 0)
    lane = iota((8, LANES), 1)
    even = (sub & 1) == 0

    def wide(row):
        return jnp.broadcast_to(row, (8, LANES))

    scale = [
        jnp.where((cross + d >= 0) & (cross + d < n_cross), F32(DAMPING / 6.0), F32(0.0)) for d in range(-2, 3)
    ]
    tiles = (far_left_ref, from_left_ref.at[16], coarse_ref, from_right_ref.at[16], far_right_ref)
    ids = [wide(t[4:5]) for t in tiles]
    masks = [wide(t[5:6]) for t in tiles]
    owner = jnp.where(sub < 2, ids[1], jnp.where(sub < 4, ids[2], ids[3]))
    strip = []
    for d in range(5):
        chosen = (ids[d] == owner) & (masks[d] > 0.5)
        for j in range(2):
            cells = jnp.where(even, wide(tiles[d][j : j + 1]), wide(tiles[d][2 + j : 3 + j]))
            strip.append(jnp.where(chosen, cells, 0.0))
    e = [scale[j // 2] * strip[j] for j in range(10)]
    for step in range(1, 4):
        new = list(e)
        for j in range(step, 10 - step):
            beside = e[j - 1] + e[j + 1]
            beside = beside + jnp.where(even, pltpu.roll(e[j], 7, 0), pltpu.roll(e[j], 1, 0))
            beside = beside + jnp.where(lane < CUBE, 0.0, pltpu.roll(e[j], CUBE, 1))
            beside = beside + jnp.where(lane >= LANES - CUBE, 0.0, pltpu.roll(e[j], LANES - CUBE, 1))
            new[j] = (1.0 - DAMPING) * e[j] + scale[j // 2] * (strip[j] + beside)
        e = new
    mask = jnp.where(
        sub < 2, jnp.where(has_left, masks[1], 0.0), jnp.where(sub < 4, masks[2], jnp.where(has_right, masks[3], 0.0))
    )
    for j in range(3, 7):
        e_ref[j - 3] = e[j] * mask

    in_left = (sub >= 3) & (sub < 7) & has_left
    in_right = (sub >= 1) & (sub < 5) & has_right
    for i in range(2):
        first, second = wide(e_ref[1, 2 + i : 3 + i]), wide(e_ref[2, 2 + i : 3 + i])
        own = jnp.concatenate([first, first, second, second], axis=0)
        beside = wide(e_ref[0, i : i + 1]), wide(e_ref[3, 4 + i : 5 + i])
        for k in range(CUBE):
            r = i * CUBE + k
            source = ends_ref.at[0, r] if r < 3 else (inner_ref.at[r] if r < N - 3 else ends_ref.at[1, r - N + 3])
            v_ref[r, 8 : 8 + N] = source[8 : 8 + N] + own
            left, right = from_left_ref[k], from_right_ref[k]
            if i == 1:
                left, right = pltpu.roll(left, 4, 0), pltpu.roll(right, 4, 0)
            left = jnp.where(in_left, left, jnp.where(sub == 7, source[0:8], 0.0))
            right = jnp.where(in_right, right, jnp.where(sub == 0, source[8 + N :], 0.0))
            v_ref[r, 0:8] = left + beside[0]
            v_ref[r, 8 + N :] = right + beside[1]
    for target, start in ((up_ref, 0), (down_ref, N - REACH)):
        for k in range(REACH):
            target[k, 0:N] = v_ref[start + k, 8 : 8 + N]
            target[k, N:] = jnp.where(sub < 4, v_ref[start + k, 8 + N :], v_ref[start + k, 0:8])


def second_inner_kernel(
    b_ref, s_ref, v_in_ref, ww_ref, wwb_ref, saved_ref, pressure_hbm, residual_hbm, v_ref, residual_ref, sems
):
    for r in range(N):
        v_ref[r] = v_in_ref[r]
    inner_sweeps(v_ref, ww_ref, wwb_ref, saved_ref, 4)
    low, high = 4, N - 4
    first = pltpu.make_async_copy(
        v_ref.at[pl.ds(low, high - low), pl.ds(8, N), :], pressure_hbm.at[pl.ds(low, high - low)], sems.at[0]
    )
    first.start()
    low, high = 5, N - 5
    for r in range(low, high):
        residual_ref[r - low] = fine_residual(v_ref[r - 1], v_ref[r], v_ref[r + 1], b_ref[r], s_ref[r])
    second = pltpu.make_async_copy(residual_ref, residual_hbm.at[pl.ds(low, high - low)], sems.at[1])
    second.start()
    first.wait()
    second.wait()


def second_outer_kernel(
    b_ref, s_ref, v_ref, ww_ref, wwb_ref, halo_ref, saved_ref, above_ref, below_ref, pressure_in, residual_in,
    pressure_hbm, residual_hbm, pressure_ref, residual_ref, sems,
):
    span = lax.axis_index("span")
    inside = (span > 0, span < lax.axis_size("span") - 1)
    sub = iota((8, LANES), 0)

    def coefficients(r):
        if 0 <= r < N:
            return ww_ref[r], wwb_ref[r]
        side, k = (0, r + HALO) if r < 0 else (1, r - N)
        return halo_ref[side, 0, k], halo_ref[side, 1, k]

    copies = []
    for side, source in enumerate((above_ref, below_ref)):
        outside = []
        for k in range(REACH):
            beside = source[k, N:]
            left = jnp.where((sub >= 4) & inside[side], beside, 0.0)
            right = jnp.where((sub < 4) & inside[side], beside, 0.0)
            outside.append(jnp.concatenate([left, jnp.where(inside[side], source[k, 0:N], 0.0), right], axis=0))
        if side == 0:
            rows, start = outside + [v_ref[0], v_ref[1]], -REACH
        else:
            rows, start = [v_ref[N - 2], v_ref[N - 1]] + outside, N - 2
        rows, start = outer_sweeps(rows, start, 4, side, coefficients, saved_ref)
        for k in range(4):
            pressure_ref[side, k] = rows[k + 1 + side][8 : 8 + N]
        for i in range(1, 6):
            r = start + i
            residual_ref[side, i - 1] = fine_residual(*rows[i - 1 : i + 2], b_ref[r], s_ref[r])
        for ref, hbm, count in ((pressure_ref, pressure_hbm, 4), (residual_ref, residual_hbm, 5)):
            place = pl.ds(0 if side == 0 else N - count, count)
            copies.append(pltpu.make_async_copy(ref.at[side], hbm.at[place], sems.at[len(copies)]))
            copies[-1].start()
    for copy in copies:
        copy.wait()


VMEM = pl.BlockSpec(memory_space=pltpu.VMEM)
HBM = pl.BlockSpec(memory_space=pltpu.HBM)


def call(kernel, outs, args, scratch=(), ins=None, out_specs=None, ops=0, room=32, aliases=None):
    size = 4 * sum(math.prod(s) for s in outs)
    return pl.pallas_call(
        kernel,
        out_shape=[jax.ShapeDtypeStruct(s, F32) for s in outs],
        in_specs=ins or [VMEM] * len(args),
        out_specs=out_specs or [VMEM] * len(outs),
        scratch_shapes=[pltpu.VMEM(s, F32) if isinstance(s, tuple) else s for s in scratch],
        input_output_aliases=aliases or {},
        compiler_params=pltpu.CompilerParams(vmem_limit_bytes=room * 1024 * 1024),
        cost_estimate=pl.CostEstimate(flops=ops, bytes_accessed=2 * size, transcendentals=0),
    )(*args)


def shifted(block, axis, step):
    count = lax.axis_size(axis)
    pairs = [(i, (i + step) % count) for i in range(count)]
    return lax.ppermute(block, axis, [p for p in pairs if axis == "span" or p[1] - p[0] == step])


def on_device(right_side, shift, tile_mask, owner_lists, owner_ids):
    block, wide, edge = (N, N, LANES), (N, WIDE, LANES), (N, 8, LANES)
    sems = pltpu.SemaphoreType.DMA
    right, left = call(
        edges_kernel, [edge, edge], [right_side, shift], scratch=[edge, edge, edge, edge, sems((4,))],
        ins=[HBM] * 2, room=60,
    )
    b, s, right, left = lax.optimization_barrier((right_side, shift, right, left))
    from_left = shifted(right, "cross", 1)
    from_right = shifted(left, "cross", -1)
    w, wb, info = call(
        coefficients_kernel, [block, block, (8, LANES)], [b, s, tile_mask, owner_ids], ops=2**20
    )
    rows = (2, HALO, N + 8, LANES)
    down, up = call(rows_kernel, [rows, rows], [w, wb, from_left, from_right])
    above = shifted(down, "span", 1)
    below = shifted(up, "span", -1)
    v, ww, wwb, saved, partial = call(
        first_inner_kernel,
        [wide, wide, wide, (2, 3, 2, WIDE, LANES), (2, N, LANES)],
        [b, s, w, wb, from_left, from_right],
        ops=2**23,
    )
    ends, halo, right, left, coarse = call(
        first_outer_kernel,
        [(2, 3, WIDE, LANES), (2, 2, HALO, WIDE, LANES), (17, 8, LANES), (17, 8, LANES), (8, LANES)],
        [b, s, v, ww, wwb, saved, partial, above, below, info],
    )
    far_left = shifted(coarse, "cross", 2)
    far_right = shifted(coarse, "cross", -2)
    from_left = shifted(right, "cross", 1)
    from_right = shifted(left, "cross", -1)
    rows = (REACH, N + 8, LANES)
    v, down, up = call(
        correct_kernel,
        [wide, rows, rows],
        [v, ends, coarse, far_left, far_right, from_left, from_right],
        scratch=[(4, 8, LANES)],
    )
    above = shifted(down, "span", 1)
    below = shifted(up, "span", -1)
    saved, pressure, residual = call(
        second_inner_kernel,
        [(2, 4, 2, WIDE, LANES), block, block],
        [b, s, v, ww, wwb],
        scratch=[wide, (N - 10, N, LANES), sems((2,))],
        out_specs=[VMEM, HBM, HBM],
        ops=2**23,
    )
    return tuple(
        call(
            second_outer_kernel,
            [block, block],
            [b, s, v, ww, wwb, halo, saved, above, below, pressure, residual],
            scratch=[(2, 4, N, LANES), (2, 5, N, LANES), sems((4,))],
            ins=[VMEM] * 9 + [HBM] * 2,
            out_specs=[HBM, HBM],
            aliases={9: 0, 10: 1},
        )
    )


def solution(mesh):
    return jax.shard_map(
        on_device,
        mesh=mesh,
        in_specs=(
            P("span", "cross", None),
            P("span", "cross", None),
            P("span", "cross"),
            P("span", "cross", None),
            P("span", "cross"),
        ),
        out_specs=(P("span", "cross", None), P("span", "cross", None)),
        check_vma=False,
    )
```

```python
import math

import jax
import jax.numpy as jnp
from jax import lax
from jax.experimental import pallas as pl
from jax.experimental.pallas import tpu as pltpu
from jax.sharding import PartitionSpec as P

DAMPING = 0.8
N = 32
LANES = 128
WIDE = N + 16
HALO = 4
REACH = 5
ROWS_W = N + 2 * HALO
ROWS_V = N + 2 * REACH
CUBE = 16
F32 = jnp.float32


def iota(shape, axis):
    return lax.broadcasted_iota(jnp.int32, shape, axis)


def neighbours(prev, cur, nxt):
    cells = cur.shape[0]
    lane = iota(cur.shape, 1)
    low = jnp.where(lane == 0, 0.0, pltpu.roll(cur, 1, 1))
    high = jnp.where(lane == LANES - 1, 0.0, pltpu.roll(cur, LANES - 1, 1))
    beside = pltpu.roll(cur, 1, 0) + pltpu.roll(cur, cells - 1, 0)
    return (prev + nxt) + beside + (low + high)


def swept(prev, cur, nxt, w, wb):
    return (1.0 - DAMPING) * cur + (wb + w * neighbours(prev, cur, nxt))


def inner_sweeps(v_ref, w_ref, wb_ref, saved_ref, count):
    def one(step, carry):
        prev, cur = v_ref[0], v_ref[1]
        for r in range(1, N - 1):
            nxt = v_ref[r + 1]
            v_ref[r] = swept(prev, cur, nxt, w_ref[r], wb_ref[r])
            prev, cur = cur, nxt
        for k in range(2):
            saved_ref[0, step, k] = v_ref[step + 1 + k]
            saved_ref[1, step, k] = v_ref[N - 3 - step + k]
        return carry

    lax.fori_loop(0, count, one, 0)


def outer_sweeps(rows, first, count, side, coefficients, saved_ref):
    for step in range(count):
        new = [swept(*rows[i : i + 3], *coefficients(first + 1 + i)) for i in range(len(rows) - 2)]
        saved = [saved_ref[side, step, k] for k in range(2)]
        rows, first = (new + saved, first + 1) if side == 0 else (saved + new, first - 1)
    return rows, first


def fine_residual(prev, cur, nxt, b, s):
    own = slice(8, 8 + N)
    return b - ((6.0 + s) * cur[own] - neighbours(prev, cur, nxt)[own])


def edges_kernel(b_ref, s_ref, right_ref, left_ref, b_left, b_right, s_left, s_right, sems):
    copies = [
        pltpu.make_async_copy(source.at[:, pl.ds(start, 8), :], target, sems.at[n])
        for n, (source, start, target) in enumerate(
            ((s_ref, N - 8, s_right), (b_ref, N - 8, b_right), (s_ref, 0, s_left), (b_ref, 0, b_left))
        )
    ]
    for copy in copies:
        copy.start()
    sub = iota((8, LANES), 0)
    copies[0].wait()
    copies[1].wait()
    for r in range(N):
        w = DAMPING / (6.0 + s_right[r])
        right_ref[r] = jnp.where(sub < 4, pltpu.roll(w, 4, 0), w * b_right[r])
    copies[2].wait()
    copies[3].wait()
    for r in range(N):
        w = DAMPING / (6.0 + s_left[r])
        left_ref[r] = jnp.where(sub < 4, w, pltpu.roll(w * b_left[r], 4, 0))


def coefficients_kernel(b_ref, s_ref, mask_ref, id_ref, w_ref, wb_ref, info_ref):
    for r in range(N):
        w = DAMPING / (6.0 + s_ref[r])
        w_ref[r] = w
        wb_ref[r] = w * b_ref[r]
    sub = iota((8, LANES), 0)
    number = jnp.broadcast_to(id_ref[...].astype(F32), (8, LANES))
    mask = jnp.broadcast_to(mask_ref[...].astype(F32), (8, LANES))
    info_ref[...] = jnp.where(sub == 4, number, jnp.where(sub == 5, mask, 0.0))


def beside_of(left_msg, right_msg):
    sub = iota((8, LANES), 0)
    w = jnp.where(sub < 4, right_msg, pltpu.roll(left_msg, 4, 0))
    wb = jnp.where(sub < 4, pltpu.roll(right_msg, 4, 0), left_msg)
    return w, wb


def rows_kernel(w_ref, wb_ref, from_left_ref, from_right_ref, down_ref, up_ref):
    for target, start in ((up_ref, 0), (down_ref, N - HALO)):
        for k in range(HALO):
            r = start + k
            sides = beside_of(from_left_ref[r], from_right_ref[r])
            for a, ref in enumerate((w_ref, wb_ref)):
                target[a, k, 0:N] = ref[r]
                target[a, k, N:] = sides[a]


def first_inner_kernel(
    b_ref, s_ref, w_ref, wb_ref, from_left_ref, from_right_ref, v_ref, ww_ref, wwb_ref, saved_ref, partial_ref
):
    cross = lax.axis_index("cross")
    sub = iota((8, LANES), 0)
    in_left, in_right = (sub >= 4) & (cross > 0), (sub < 4) & (cross < lax.axis_size("cross") - 1)
    for r in range(N):
        w_side, wb_side = beside_of(from_left_ref[r], from_right_ref[r])
        for ref, own, side in ((ww_ref, w_ref[r], w_side), (wwb_ref, wb_ref[r], wb_side)):
            ref[r, 0:8] = jnp.where(in_left, side, 0.0)
            ref[r, 8 : 8 + N] = own
            ref[r, 8 + N :] = jnp.where(in_right, side, 0.0)
        v_ref[r] = wwb_ref[r]
    inner_sweeps(v_ref, ww_ref, wwb_ref, saved_ref, 3)
    for part in range(2):
        total = jnp.zeros((N, LANES), F32)
        for r in range(4 + 12 * part, 16 + 12 * part):
            total = total + fine_residual(v_ref[r - 1], v_ref[r], v_ref[r + 1], b_ref[r], s_ref[r])
        partial_ref[part] = total


def first_outer_kernel(
    b_ref, s_ref, v_ref, ww_ref, wwb_ref, saved_ref, partial_ref, below_ref, above_ref, info_ref,
    ends_ref, halo_ref, right_ref, left_ref, coarse_ref,
):
    span, cross = lax.axis_index("span"), lax.axis_index("cross")
    sub = iota((8, LANES), 0)
    in_left, in_right = (sub >= 4) & (cross > 0), (sub < 4) & (cross < lax.axis_size("cross") - 1)
    inside = (span > 0, span < lax.axis_size("span") - 1)
    for side, source in enumerate((above_ref, below_ref)):
        for a in range(2):
            for k in range(HALO):
                beside = source[a, k, N:]
                halo_ref[side, a, k, 0:8] = jnp.where(in_left & inside[side], beside, 0.0)
                halo_ref[side, a, k, 8 : 8 + N] = jnp.where(inside[side], source[a, k, 0:N], 0.0)
                halo_ref[side, a, k, 8 + N :] = jnp.where(in_right & inside[side], beside, 0.0)

    def coefficients(r):
        if 0 <= r < N:
            return ww_ref[r], wwb_ref[r]
        side, k = (0, r + HALO) if r < 0 else (1, r - N)
        return halo_ref[side, 0, k], halo_ref[side, 1, k]

    tile = info_ref[...]
    for side in range(2):
        start = -HALO if side == 0 else N - 2
        rows, start = outer_sweeps(
            [coefficients(r)[1] for r in range(start, start + HALO + 2)], start, 3, side, coefficients, saved_ref
        )
        total = partial_ref[side]
        for i in range(1, 5):
            r = start + i
            total = total + fine_residual(*rows[i - 1 : i + 2], b_ref[r], s_ref[r])
        for half in range(2):
            row = jnp.sum(total[half * CUBE : (half + 1) * CUBE], axis=0, keepdims=True)
            tile = jnp.where(sub == 2 * side + half, row, tile)
        for k in range(3):
            ends_ref[side, k] = rows[k + 1 + side]
    lane = iota((8, LANES), 1)
    cells = tile
    for step in (1, 2, 4, 8):
        cells = cells + jnp.where((lane & step) == 0, pltpu.roll(cells, LANES - step, 1), pltpu.roll(cells, step, 1))
    tile = jnp.where(sub < 4, cells / float(CUBE), tile)
    coarse_ref[...] = tile
    right_ref[16] = tile
    left_ref[16] = tile

    def pressure(r):
        return ends_ref.at[0, r] if r < 3 else (v_ref.at[r] if r < N - 3 else ends_ref.at[1, r - N + 3])

    for k in range(16):
        a, c = pressure(k), pressure(16 + k)
        right_ref[k] = jnp.where((sub >= 3) & (sub < 7), a[N : N + 8], pltpu.roll(c[N : N + 8], 4, 0))
        left_ref[k] = jnp.where((sub >= 1) & (sub < 5), a[8:16], pltpu.roll(c[8:16], 4, 0))


def correct_kernel(
    inner_ref, ends_ref, coarse_ref, far_right_ref, far_left_ref, from_left_ref, from_right_ref, v_ref, down_ref, up_ref, e_ref
):
    cross, n_cross = lax.axis_index("cross"), lax.axis_size("cross")
    has_left, has_right = cross > 0, cross < n_cross - 1
    sub = iota((8, LANES), 0)
    lane = iota((8, LANES), 1)
    even = (sub & 1) == 0

    def wide(row):
        return jnp.broadcast_to(row, (8, LANES))

    scale = [
        jnp.where((cross + d >= 0) & (cross + d < n_cross), F32(DAMPING / 6.0), F32(0.0)) for d in range(-2, 3)
    ]
    tiles = (far_left_ref, from_left_ref.at[16], coarse_ref, from_right_ref.at[16], far_right_ref)
    ids = [wide(t[4:5]) for t in tiles]
    masks = [wide(t[5:6]) for t in tiles]
    owner = jnp.where(sub < 2, ids[1], jnp.where(sub < 4, ids[2], ids[3]))
    strip = []
    for d in range(5):
        chosen = (ids[d] == owner) & (masks[d] > 0.5)
        for j in range(2):
            cells = jnp.where(even, wide(tiles[d][j : j + 1]), wide(tiles[d][2 + j : 3 + j]))
            strip.append(jnp.where(chosen, cells, 0.0))
    e = [scale[j // 2] * strip[j] for j in range(10)]
    for step in range(1, 4):
        new = list(e)
        for j in range(step, 10 - step):
            beside = e[j - 1] + e[j + 1]
            beside = beside + jnp.where(even, pltpu.roll(e[j], 7, 0), pltpu.roll(e[j], 1, 0))
            beside = beside + jnp.where(lane < CUBE, 0.0, pltpu.roll(e[j], CUBE, 1))
            beside = beside + jnp.where(lane >= LANES - CUBE, 0.0, pltpu.roll(e[j], LANES - CUBE, 1))
            new[j] = (1.0 - DAMPING) * e[j] + scale[j // 2] * (strip[j] + beside)
        e = new
    mask = jnp.where(
        sub < 2, jnp.where(has_left, masks[1], 0.0), jnp.where(sub < 4, masks[2], jnp.where(has_right, masks[3], 0.0))
    )
    for j in range(3, 7):
        e_ref[j - 3] = e[j] * mask

    in_left = (sub >= 3) & (sub < 7) & has_left
    in_right = (sub >= 1) & (sub < 5) & has_right
    for i in range(2):
        first, second = wide(e_ref[1, 2 + i : 3 + i]), wide(e_ref[2, 2 + i : 3 + i])
        own = jnp.concatenate([first, first, second, second], axis=0)
        beside = wide(e_ref[0, i : i + 1]), wide(e_ref[3, 4 + i : 5 + i])
        for k in range(CUBE):
            r = i * CUBE + k
            source = ends_ref.at[0, r] if r < 3 else (inner_ref.at[r] if r < N - 3 else ends_ref.at[1, r - N + 3])
            v_ref[r, 8 : 8 + N] = source[8 : 8 + N] + own
            left, right = from_left_ref[k], from_right_ref[k]
            if i == 1:
                left, right = pltpu.roll(left, 4, 0), pltpu.roll(right, 4, 0)
            left = jnp.where(in_left, left, jnp.where(sub == 7, source[0:8], 0.0))
            right = jnp.where(in_right, right, jnp.where(sub == 0, source[8 + N :], 0.0))
            v_ref[r, 0:8] = left + beside[0]
            v_ref[r, 8 + N :] = right + beside[1]
    for target, start in ((up_ref, 0), (down_ref, N - REACH)):
        for k in range(REACH):
            target[k, 0:N] = v_ref[start + k, 8 : 8 + N]
            target[k, N:] = jnp.where(sub < 4, v_ref[start + k, 8 + N :], v_ref[start + k, 0:8])


def second_inner_kernel(
    b_ref, s_ref, v_in_ref, ww_ref, wwb_ref, saved_ref, pressure_hbm, residual_hbm, v_ref, residual_ref, sems
):
    for r in range(N):
        v_ref[r] = v_in_ref[r]
    inner_sweeps(v_ref, ww_ref, wwb_ref, saved_ref, 4)
    low, high = 4, N - 4
    first = pltpu.make_async_copy(
        v_ref.at[pl.ds(low, high - low), pl.ds(8, N), :], pressure_hbm.at[pl.ds(low, high - low)], sems.at[0]
    )
    first.start()
    low, high = 5, N - 5
    for r in range(low, high):
        residual_ref[r - low] = fine_residual(v_ref[r - 1], v_ref[r], v_ref[r + 1], b_ref[r], s_ref[r])
    second = pltpu.make_async_copy(residual_ref, residual_hbm.at[pl.ds(low, high - low)], sems.at[1])
    second.start()
    first.wait()
    second.wait()


def second_outer_kernel(
    b_ref, s_ref, v_ref, ww_ref, wwb_ref, halo_ref, saved_ref, below_ref, above_ref, pressure_in, residual_in,
    pressure_hbm, residual_hbm, pressure_ref, residual_ref, sems,
):
    span = lax.axis_index("span")
    inside = (span > 0, span < lax.axis_size("span") - 1)
    sub = iota((8, LANES), 0)

    def coefficients(r):
        if 0 <= r < N:
            return ww_ref[r], wwb_ref[r]
        side, k = (0, r + HALO) if r < 0 else (1, r - N)
        return halo_ref[side, 0, k], halo_ref[side, 1, k]

    copies = []
    for side, source in enumerate((above_ref, below_ref)):
        outside = []
        for k in range(REACH):
            beside = source[k, N:]
            left = jnp.where((sub >= 4) & inside[side], beside, 0.0)
            right = jnp.where((sub < 4) & inside[side], beside, 0.0)
            outside.append(jnp.concatenate([left, jnp.where(inside[side], source[k, 0:N], 0.0), right], axis=0))
        if side == 0:
            rows, start = outside + [v_ref[0], v_ref[1]], -REACH
        else:
            rows, start = [v_ref[N - 2], v_ref[N - 1]] + outside, N - 2
        rows, start = outer_sweeps(rows, start, 4, side, coefficients, saved_ref)
        for k in range(4):
            pressure_ref[side, k] = rows[k + 1 + side][8 : 8 + N]
        for i in range(1, 6):
            r = start + i
            residual_ref[side, i - 1] = fine_residual(*rows[i - 1 : i + 2], b_ref[r], s_ref[r])
        for ref, hbm, count in ((pressure_ref, pressure_hbm, 4), (residual_ref, residual_hbm, 5)):
            place = pl.ds(0 if side == 0 else N - count, count)
            copies.append(pltpu.make_async_copy(ref.at[side], hbm.at[place], sems.at[len(copies)]))
            copies[-1].start()
    for copy in copies:
        copy.wait()


VMEM = pl.BlockSpec(memory_space=pltpu.VMEM)
HBM = pl.BlockSpec(memory_space=pltpu.HBM)


def call(kernel, outs, args, scratch=(), ins=None, out_specs=None, ops=0, room=32, aliases=None):
    size = 4 * sum(math.prod(s) for s in outs)
    return pl.pallas_call(
        kernel,
        out_shape=[jax.ShapeDtypeStruct(s, F32) for s in outs],
        in_specs=ins or [VMEM] * len(args),
        out_specs=out_specs or [VMEM] * len(outs),
        scratch_shapes=[pltpu.VMEM(s, F32) if isinstance(s, tuple) else s for s in scratch],
        input_output_aliases=aliases or {},
        compiler_params=pltpu.CompilerParams(vmem_limit_bytes=room * 1024 * 1024),
        cost_estimate=pl.CostEstimate(flops=ops, bytes_accessed=2 * size, transcendentals=0),
    )(*args)


def shifted(block, axis, step):
    count = lax.axis_size(axis)
    pairs = [(i, (i + step) % count) for i in range(count)]
    return lax.ppermute(block, axis, [p for p in pairs if axis == "span" or p[1] - p[0] == step])


def on_device(right_side, shift, tile_mask, owner_lists, owner_ids):
    block, wide, edge = (N, N, LANES), (N, WIDE, LANES), (N, 8, LANES)
    sems = pltpu.SemaphoreType.DMA
    right, left = call(
        edges_kernel, [edge, edge], [right_side, shift], scratch=[edge, edge, edge, edge, sems((4,))],
        ins=[HBM] * 2, room=60,
    )
    b, s, right, left = lax.optimization_barrier((right_side, shift, right, left))
    from_left = shifted(right, "cross", 1)
    from_right = shifted(left, "cross", -1)
    w, wb, info = call(
        coefficients_kernel, [block, block, (8, LANES)], [b, s, tile_mask, owner_ids], ops=2**20
    )
    rows = (2, HALO, N + 8, LANES)
    down, up = call(rows_kernel, [rows, rows], [w, wb, from_left, from_right])
    above = shifted(down, "span", 1)
    below = shifted(up, "span", -1)
    v, ww, wwb, saved, partial = call(
        first_inner_kernel,
        [wide, wide, wide, (2, 3, 2, WIDE, LANES), (2, N, LANES)],
        [b, s, w, wb, from_left, from_right],
        ops=2**23,
    )
    ends, halo, right, left, coarse = call(
        first_outer_kernel,
        [(2, 3, WIDE, LANES), (2, 2, HALO, WIDE, LANES), (17, 8, LANES), (17, 8, LANES), (8, LANES)],
        [b, s, v, ww, wwb, saved, partial, below, above, info],
    )
    far_left = shifted(coarse, "cross", 2)
    far_right = shifted(coarse, "cross", -2)
    from_left = shifted(right, "cross", 1)
    from_right = shifted(left, "cross", -1)
    rows = (REACH, N + 8, LANES)
    v, down, up = call(
        correct_kernel,
        [wide, rows, rows],
        [v, ends, coarse, far_right, far_left, from_left, from_right],
        scratch=[(4, 8, LANES)],
    )
    above = shifted(down, "span", 1)
    below = shifted(up, "span", -1)
    saved, pressure, residual = call(
        second_inner_kernel,
        [(2, 4, 2, WIDE, LANES), block, block],
        [b, s, v, ww, wwb],
        scratch=[wide, (N - 10, N, LANES), sems((2,))],
        out_specs=[VMEM, HBM, HBM],
        ops=2**23,
    )
    return tuple(
        call(
            second_outer_kernel,
            [block, block],
            [b, s, v, ww, wwb, halo, saved, below, above, pressure, residual],
            scratch=[(2, 4, N, LANES), (2, 5, N, LANES), sems((4,))],
            ins=[VMEM] * 9 + [HBM] * 2,
            out_specs=[HBM, HBM],
            aliases={9: 0, 10: 1},
        )
    )


def solution(mesh):
    return jax.shard_map(
        on_device,
        mesh=mesh,
        in_specs=(
            P("span", "cross", None),
            P("span", "cross", None),
            P("span", "cross"),
            P("span", "cross", None),
            P("span", "cross"),
        ),
        out_specs=(P("span", "cross", None), P("span", "cross", None)),
        check_vma=False,
    )
```

```python
import math

import jax
import jax.numpy as jnp
from jax import lax
from jax.experimental import pallas as pl
from jax.experimental.pallas import tpu as pltpu
from jax.sharding import PartitionSpec as P

DAMPING = 0.8
N = 32
LANES = 128
WIDE = N + 16
HALO = 4
REACH = 5
ROWS_W = N + 2 * HALO
ROWS_V = N + 2 * REACH
CUBE = 16
F32 = jnp.float32


def iota(shape, axis):
    return lax.broadcasted_iota(jnp.int32, shape, axis)


def neighbours(prev, cur, nxt):
    cells = cur.shape[0]
    lane = iota(cur.shape, 1)
    low = jnp.where(lane == 0, 0.0, pltpu.roll(cur, 1, 1))
    high = jnp.where(lane == LANES - 1, 0.0, pltpu.roll(cur, LANES - 1, 1))
    beside = pltpu.roll(cur, 1, 0) + pltpu.roll(cur, cells - 1, 0)
    return (prev + nxt) + beside + (low + high)


def swept(prev, cur, nxt, w, wb):
    return (1.0 - DAMPING) * cur + (wb + w * neighbours(prev, cur, nxt))


def inner_sweeps(v_ref, w_ref, wb_ref, saved_ref, count):
    def one(step, carry):
        prev, cur = v_ref[0], v_ref[1]
        for r in range(1, N - 1):
            nxt = v_ref[r + 1]
            v_ref[r] = swept(prev, cur, nxt, w_ref[r], wb_ref[r])
            prev, cur = cur, nxt
        for k in range(2):
            saved_ref[0, step, k] = v_ref[step + 1 + k]
            saved_ref[1, step, k] = v_ref[N - 3 - step + k]
        return carry

    lax.fori_loop(0, count, one, 0)


def outer_sweeps(ends, count, coefficients, saved_ref):
    for step in range(count):
        later = []
        for side, (rows, first) in enumerate(ends):
            new = [swept(*rows[i : i + 3], *coefficients(first + 1 + i)) for i in range(len(rows) - 2)]
            saved = [saved_ref[side, step, k] for k in range(2)]
            later.append((new + saved, first + 1) if side == 0 else (saved + new, first - 1))
        ends = later
    return ends


def fine_residual(prev, cur, nxt, b, s):
    own = slice(8, 8 + N)
    return b - ((6.0 + s) * cur[own] - neighbours(prev, cur, nxt)[own])


def edges_kernel(b_ref, s_ref, right_ref, left_ref, b_left, b_right, s_left, s_right, sems):
    copies = [
        pltpu.make_async_copy(source.at[:, pl.ds(start, 4), :], target.at[:, pl.ds(start % 8, 4), :], sems.at[n])
        for n, (source, start, target) in enumerate(
            ((s_ref, N - 4, s_right), (b_ref, N - 4, b_right), (s_ref, 0, s_left), (b_ref, 0, b_left))
        )
    ]
    for copy in copies:
        copy.start()
    sub = iota((8, LANES), 0)
    copies[0].wait()
    copies[1].wait()
    for r in range(N):
        w = DAMPING / (6.0 + s_right[r])
        right_ref[r] = jnp.where(sub < 4, pltpu.roll(w, 4, 0), w * b_right[r])
    copies[2].wait()
    copies[3].wait()
    for r in range(N):
        w = DAMPING / (6.0 + s_left[r])
        left_ref[r] = jnp.where(sub < 4, w, pltpu.roll(w * b_left[r], 4, 0))


def coefficients_kernel(b_ref, s_ref, mask_ref, id_ref, w_ref, wb_ref, info_ref):
    for r in range(N):
        w = DAMPING / (6.0 + s_ref[r])
        w_ref[r] = w
        wb_ref[r] = w * b_ref[r]
    sub = iota((8, LANES), 0)
    number = jnp.broadcast_to(id_ref[...].astype(F32), (8, LANES))
    mask = jnp.broadcast_to(mask_ref[...].astype(F32), (8, LANES))
    info_ref[...] = jnp.where(sub == 4, number, jnp.where(sub == 5, mask, 0.0))


def beside_of(left_msg, right_msg):
    sub = iota((8, LANES), 0)
    w = jnp.where(sub < 4, right_msg, pltpu.roll(left_msg, 4, 0))
    wb = jnp.where(sub < 4, pltpu.roll(right_msg, 4, 0), left_msg)
    return w, wb


def rows_kernel(w_ref, wb_ref, from_left_ref, from_right_ref, down_ref, up_ref):
    for target, start in ((up_ref, 0), (down_ref, N - HALO)):
        for k in range(HALO):
            r = start + k
            sides = beside_of(from_left_ref[r], from_right_ref[r])
            for a, ref in enumerate((w_ref, wb_ref)):
                target[a, k, 0:N] = ref[r]
                target[a, k, N:] = sides[a]


def first_inner_kernel(
    b_ref, s_ref, w_ref, wb_ref, from_left_ref, from_right_ref, v_ref, ww_ref, wwb_ref, saved_ref, partial_ref
):
    cross = lax.axis_index("cross")
    sub = iota((8, LANES), 0)
    in_left, in_right = (sub >= 4) & (cross > 0), (sub < 4) & (cross < lax.axis_size("cross") - 1)
    for r in range(N):
        w_side, wb_side = beside_of(from_left_ref[r], from_right_ref[r])
        for ref, own, side in ((ww_ref, w_ref[r], w_side), (wwb_ref, wb_ref[r], wb_side)):
            ref[r, 0:8] = jnp.where(in_left, side, 0.0)
            ref[r, 8 : 8 + N] = own
            ref[r, 8 + N :] = jnp.where(in_right, side, 0.0)
        v_ref[r] = wwb_ref[r]
    inner_sweeps(v_ref, ww_ref, wwb_ref, saved_ref, 3)
    for part in range(2):
        total = jnp.zeros((N, LANES), F32)
        for r in range(4 + 12 * part, 16 + 12 * part):
            total = total + fine_residual(v_ref[r - 1], v_ref[r], v_ref[r + 1], b_ref[r], s_ref[r])
        partial_ref[part] = total


def first_outer_kernel(
    b_ref, s_ref, v_ref, ww_ref, wwb_ref, saved_ref, partial_ref, below_ref, above_ref, info_ref,
    ends_ref, halo_ref, right_ref, left_ref, coarse_ref,
):
    span, cross = lax.axis_index("span"), lax.axis_index("cross")
    sub = iota((8, LANES), 0)
    in_left, in_right = (sub >= 4) & (cross > 0), (sub < 4) & (cross < lax.axis_size("cross") - 1)
    inside = (span > 0, span < lax.axis_size("span") - 1)
    for side, source in enumerate((above_ref, below_ref)):
        for a in range(2):
            for k in range(HALO):
                beside = source[a, k, N:]
                halo_ref[side, a, k, 0:8] = jnp.where(in_left & inside[side], beside, 0.0)
                halo_ref[side, a, k, 8 : 8 + N] = jnp.where(inside[side], source[a, k, 0:N], 0.0)
                halo_ref[side, a, k, 8 + N :] = jnp.where(in_right & inside[side], beside, 0.0)

    def coefficients(r):
        if 0 <= r < N:
            return ww_ref[r], wwb_ref[r]
        side, k = (0, r + HALO) if r < 0 else (1, r - N)
        return halo_ref[side, 0, k], halo_ref[side, 1, k]

    tile = info_ref[...]
    ends = outer_sweeps(
        [([coefficients(r)[1] for r in range(start, start + HALO + 2)], start) for start in (-HALO, N - 2)],
        3,
        coefficients,
        saved_ref,
    )
    for side, (rows, start) in enumerate(ends):
        total = partial_ref[side]
        for i in range(1, 5):
            r = start + i
            total = total + fine_residual(*rows[i - 1 : i + 2], b_ref[r], s_ref[r])
        for half in range(2):
            row = jnp.sum(total[half * CUBE : (half + 1) * CUBE], axis=0, keepdims=True)
            tile = jnp.where(sub == 2 * side + half, row, tile)
        for k in range(3):
            ends_ref[side, k] = rows[k + 1 + side]
    lane = iota((8, LANES), 1)
    cells = tile
    for step in (1, 2, 4, 8):
        cells = cells + jnp.where((lane & step) == 0, pltpu.roll(cells, LANES - step, 1), pltpu.roll(cells, step, 1))
    tile = jnp.where(sub < 4, cells / float(CUBE), tile)
    coarse_ref[...] = tile
    right_ref[16] = tile
    left_ref[16] = tile

    def pressure(r):
        return ends_ref.at[0, r] if r < 3 else (v_ref.at[r] if r < N - 3 else ends_ref.at[1, r - N + 3])

    for k in range(16):
        a, c = pressure(k), pressure(16 + k)
        right_ref[k] = jnp.where((sub >= 3) & (sub < 7), a[N : N + 8], pltpu.roll(c[N : N + 8], 4, 0))
        left_ref[k] = jnp.where((sub >= 1) & (sub < 5), a[8:16], pltpu.roll(c[8:16], 4, 0))


def correct_kernel(
    inner_ref, ends_ref, coarse_ref, far_right_ref, far_left_ref, from_left_ref, from_right_ref, v_ref, down_ref, up_ref, e_ref
):
    cross, n_cross = lax.axis_index("cross"), lax.axis_size("cross")
    has_left, has_right = cross > 0, cross < n_cross - 1
    sub = iota((8, LANES), 0)
    lane = iota((8, LANES), 1)
    even = (sub & 1) == 0

    def wide(row):
        return jnp.broadcast_to(row, (8, LANES))

    scale = [
        jnp.where((cross + d >= 0) & (cross + d < n_cross), F32(DAMPING / 6.0), F32(0.0)) for d in range(-2, 3)
    ]
    tiles = (far_left_ref, from_left_ref.at[16], coarse_ref, from_right_ref.at[16], far_right_ref)
    ids = [wide(t[4:5]) for t in tiles]
    masks = [wide(t[5:6]) for t in tiles]
    owner = jnp.where(sub < 2, ids[1], jnp.where(sub < 4, ids[2], ids[3]))
    strip = []
    for d in range(5):
        chosen = (ids[d] == owner) & (masks[d] > 0.5)
        for j in range(2):
            cells = jnp.where(even, wide(tiles[d][j : j + 1]), wide(tiles[d][2 + j : 3 + j]))
            strip.append(jnp.where(chosen, cells, 0.0))
    e = [scale[j // 2] * strip[j] for j in range(10)]
    for step in range(1, 4):
        new = list(e)
        for j in range(step, 10 - step):
            beside = e[j - 1] + e[j + 1]
            beside = beside + jnp.where(even, pltpu.roll(e[j], 7, 0), pltpu.roll(e[j], 1, 0))
            beside = beside + jnp.where(lane < CUBE, 0.0, pltpu.roll(e[j], CUBE, 1))
            beside = beside + jnp.where(lane >= LANES - CUBE, 0.0, pltpu.roll(e[j], LANES - CUBE, 1))
            new[j] = (1.0 - DAMPING) * e[j] + scale[j // 2] * (strip[j] + beside)
        e = new
    mask = jnp.where(
        sub < 2, jnp.where(has_left, masks[1], 0.0), jnp.where(sub < 4, masks[2], jnp.where(has_right, masks[3], 0.0))
    )
    for j in range(3, 7):
        e_ref[j - 3] = e[j] * mask

    in_left = (sub >= 3) & (sub < 7) & has_left
    in_right = (sub >= 1) & (sub < 5) & has_right
    for i in range(2):
        first, second = wide(e_ref[1, 2 + i : 3 + i]), wide(e_ref[2, 2 + i : 3 + i])
        own = jnp.concatenate([first, first, second, second], axis=0)
        beside = wide(e_ref[0, i : i + 1]), wide(e_ref[3, 4 + i : 5 + i])
        for k in range(CUBE):
            r = i * CUBE + k
            source = ends_ref.at[0, r] if r < 3 else (inner_ref.at[r] if r < N - 3 else ends_ref.at[1, r - N + 3])
            v_ref[r, 8 : 8 + N] = source[8 : 8 + N] + own
            left, right = from_left_ref[k], from_right_ref[k]
            if i == 1:
                left, right = pltpu.roll(left, 4, 0), pltpu.roll(right, 4, 0)
            left = jnp.where(in_left, left, jnp.where(sub == 7, source[0:8], 0.0))
            right = jnp.where(in_right, right, jnp.where(sub == 0, source[8 + N :], 0.0))
            v_ref[r, 0:8] = left + beside[0]
            v_ref[r, 8 + N :] = right + beside[1]
    for target, start in ((up_ref, 0), (down_ref, N - REACH)):
        for k in range(REACH):
            target[k, 0:N] = v_ref[start + k, 8 : 8 + N]
            target[k, N:] = jnp.where(sub < 4, v_ref[start + k, 8 + N :], v_ref[start + k, 0:8])


def second_inner_kernel(
    b_ref, s_ref, v_in_ref, ww_ref, wwb_ref, saved_ref, pressure_hbm, residual_hbm, v_ref, residual_ref, sems
):
    for r in range(N):
        v_ref[r] = v_in_ref[r]
    inner_sweeps(v_ref, ww_ref, wwb_ref, saved_ref, 4)
    low, high = 4, N - 4
    first = pltpu.make_async_copy(
        v_ref.at[pl.ds(low, high - low), pl.ds(8, N), :], pressure_hbm.at[pl.ds(low, high - low)], sems.at[0]
    )
    first.start()
    low = 5
    copies = [first]
    for place, count in ((5, 14), (19, 8)):
        for r in range(place, place + count):
            residual_ref[r - low] = fine_residual(v_ref[r - 1], v_ref[r], v_ref[r + 1], b_ref[r], s_ref[r])
        copies.append(
            pltpu.make_async_copy(
                residual_ref.at[pl.ds(place - low, count)], residual_hbm.at[pl.ds(place, count)], sems.at[len(copies)]
            )
        )
        copies[-1].start()
    for copy in copies:
        copy.wait()


def second_outer_kernel(
    b_ref, s_ref, v_ref, ww_ref, wwb_ref, halo_ref, saved_ref, below_ref, above_ref, pressure_in, residual_in,
    pressure_hbm, residual_hbm, pressure_ref, residual_ref, sems,
):
    span = lax.axis_index("span")
    inside = (span > 0, span < lax.axis_size("span") - 1)
    sub = iota((8, LANES), 0)

    def coefficients(r):
        if 0 <= r < N:
            return ww_ref[r], wwb_ref[r]
        side, k = (0, r + HALO) if r < 0 else (1, r - N)
        return halo_ref[side, 0, k], halo_ref[side, 1, k]

    copies, ends = [], []
    for side, source in enumerate((above_ref, below_ref)):
        outside = []
        for k in range(REACH):
            beside = source[k, N:]
            left = jnp.where((sub >= 4) & inside[side], beside, 0.0)
            right = jnp.where((sub < 4) & inside[side], beside, 0.0)
            outside.append(jnp.concatenate([left, jnp.where(inside[side], source[k, 0:N], 0.0), right], axis=0))
        ends.append((outside + [v_ref[0], v_ref[1]], -REACH) if side == 0 else ([v_ref[N - 2], v_ref[N - 1]] + outside, N - 2))
    ends = outer_sweeps(ends, 4, coefficients, saved_ref)
    for side, (rows, start) in enumerate(ends):
        for k in range(4):
            pressure_ref[side, k] = rows[k + 1 + side][8 : 8 + N]
    for side, (rows, start) in enumerate(ends):
        for i in range(1, 6):
            r = start + i
            residual_ref[side, i - 1] = fine_residual(*rows[i - 1 : i + 2], b_ref[r], s_ref[r])
    for side in range(2):
        for ref, hbm, count in ((pressure_ref, pressure_hbm, 4), (residual_ref, residual_hbm, 5)):
            place = pl.ds(0 if side == 0 else N - count, count)
            copies.append(pltpu.make_async_copy(ref.at[side], hbm.at[place], sems.at[len(copies)]))
            copies[-1].start()
    for copy in copies:
        copy.wait()


VMEM = pl.BlockSpec(memory_space=pltpu.VMEM)
HBM = pl.BlockSpec(memory_space=pltpu.HBM)


def call(kernel, outs, args, scratch=(), ins=None, out_specs=None, ops=0, room=32, aliases=None):
    size = 4 * sum(math.prod(s) for s in outs)
    return pl.pallas_call(
        kernel,
        out_shape=[jax.ShapeDtypeStruct(s, F32) for s in outs],
        in_specs=ins or [VMEM] * len(args),
        out_specs=out_specs or [VMEM] * len(outs),
        scratch_shapes=[pltpu.VMEM(s, F32) if isinstance(s, tuple) else s for s in scratch],
        input_output_aliases=aliases or {},
        compiler_params=pltpu.CompilerParams(vmem_limit_bytes=room * 1024 * 1024),
        cost_estimate=pl.CostEstimate(flops=ops, bytes_accessed=2 * size, transcendentals=0),
    )(*args)


def shifted(block, axis, step):
    count = lax.axis_size(axis)
    pairs = [(i, (i + step) % count) for i in range(count)]
    return lax.ppermute(block, axis, [p for p in pairs if axis == "span" or p[1] - p[0] == step])


def on_device(right_side, shift, tile_mask, owner_lists, owner_ids):
    block, wide, edge = (N, N, LANES), (N, WIDE, LANES), (N, 8, LANES)
    sems = pltpu.SemaphoreType.DMA
    right, left = call(
        edges_kernel, [edge, edge], [right_side, shift], scratch=[edge, edge, edge, edge, sems((4,))],
        ins=[HBM] * 2, room=60,
    )
    b, s, right, left = lax.optimization_barrier((right_side, shift, right, left))
    from_left = shifted(right, "cross", 1)
    from_right = shifted(left, "cross", -1)
    w, wb, info = call(
        coefficients_kernel, [block, block, (8, LANES)], [b, s, tile_mask, owner_ids], ops=2**20
    )
    rows = (2, HALO, N + 8, LANES)
    down, up = call(rows_kernel, [rows, rows], [w, wb, from_left, from_right])
    above = shifted(down, "span", 1)
    below = shifted(up, "span", -1)
    v, ww, wwb, saved, partial = call(
        first_inner_kernel,
        [wide, wide, wide, (2, 3, 2, WIDE, LANES), (2, N, LANES)],
        [b, s, w, wb, from_left, from_right],
        ops=2**23,
    )
    ends, halo, right, left, coarse = call(
        first_outer_kernel,
        [(2, 3, WIDE, LANES), (2, 2, HALO, WIDE, LANES), (17, 8, LANES), (17, 8, LANES), (8, LANES)],
        [b, s, v, ww, wwb, saved, partial, below, above, info],
    )
    far_left = shifted(coarse, "cross", 2)
    far_right = shifted(coarse, "cross", -2)
    from_left = shifted(right, "cross", 1)
    from_right = shifted(left, "cross", -1)
    rows = (REACH, N + 8, LANES)
    v, down, up = call(
        correct_kernel,
        [wide, rows, rows],
        [v, ends, coarse, far_right, far_left, from_left, from_right],
        scratch=[(4, 8, LANES)],
    )
    above = shifted(down, "span", 1)
    below = shifted(up, "span", -1)
    saved, pressure, residual = call(
        second_inner_kernel,
        [(2, 4, 2, WIDE, LANES), block, block],
        [b, s, v, ww, wwb],
        scratch=[wide, (N - 10, N, LANES), sems((3,))],
        out_specs=[VMEM, HBM, HBM],
        ops=2**23,
    )
    return tuple(
        call(
            second_outer_kernel,
            [block, block],
            [b, s, v, ww, wwb, halo, saved, below, above, pressure, residual],
            scratch=[(2, 4, N, LANES), (2, 5, N, LANES), sems((4,))],
            ins=[VMEM] * 9 + [HBM] * 2,
            out_specs=[HBM, HBM],
            aliases={9: 0, 10: 1},
        )
    )


def solution(mesh):
    return jax.shard_map(
        on_device,
        mesh=mesh,
        in_specs=(
            P("span", "cross", None),
            P("span", "cross", None),
            P("span", "cross"),
            P("span", "cross", None),
            P("span", "cross"),
        ),
        out_specs=(P("span", "cross", None), P("span", "cross", None)),
        check_vma=False,
    )
```

```python
import math

import jax
import jax.numpy as jnp
from jax import lax
from jax.experimental import pallas as pl
from jax.experimental.pallas import tpu as pltpu
from jax.sharding import PartitionSpec as P

DAMPING = 0.8
N = 32
LANES = 128
WIDE = N + 16
HALO = 4
REACH = 5
ROWS_W = N + 2 * HALO
ROWS_V = N + 2 * REACH
CUBE = 16
F32 = jnp.float32


def iota(shape, axis):
    return lax.broadcasted_iota(jnp.int32, shape, axis)


def neighbours(prev, cur, nxt):
    cells = cur.shape[0]
    lane = iota(cur.shape, 1)
    low = jnp.where(lane == 0, 0.0, pltpu.roll(cur, 1, 1))
    high = jnp.where(lane == LANES - 1, 0.0, pltpu.roll(cur, LANES - 1, 1))
    beside = pltpu.roll(cur, 1, 0) + pltpu.roll(cur, cells - 1, 0)
    return (prev + nxt) + beside + (low + high)


def swept(prev, cur, nxt, w, wb):
    return (1.0 - DAMPING) * cur + (wb + w * neighbours(prev, cur, nxt))


def inner_sweeps(v_ref, w_ref, wb_ref, saved_ref, count):
    def one(step, carry):
        prev, cur = v_ref[0], v_ref[1]
        for r in range(1, N - 1):
            nxt = v_ref[r + 1]
            v_ref[r] = swept(prev, cur, nxt, w_ref[r], wb_ref[r])
            prev, cur = cur, nxt
        for k in range(2):
            saved_ref[0, step, k] = v_ref[step + 1 + k]
            saved_ref[1, step, k] = v_ref[N - 3 - step + k]
        return carry

    lax.fori_loop(0, count, one, 0)


def outer_sweeps(ends, count, coefficients, saved_ref):
    for step in range(count):
        later = []
        for side, (rows, first) in enumerate(ends):
            new = [swept(*rows[i : i + 3], *coefficients(first + 1 + i)) for i in range(len(rows) - 2)]
            saved = [saved_ref[side, step, k] for k in range(2)]
            later.append((new + saved, first + 1) if side == 0 else (saved + new, first - 1))
        ends = later
    return ends


def fine_residual(prev, cur, nxt, b, s):
    own = slice(8, 8 + N)
    return b - ((6.0 + s) * cur[own] - neighbours(prev, cur, nxt)[own])


def edges_kernel(b_ref, s_ref, right_ref, left_ref, b_left, b_right, s_left, s_right, sems):
    copies = [
        pltpu.make_async_copy(source.at[:, pl.ds(start, 4), :], target.at[:, pl.ds(start % 8, 4), :], sems.at[n])
        for n, (source, start, target) in enumerate(
            ((s_ref, N - 4, s_right), (b_ref, N - 4, b_right), (s_ref, 0, s_left), (b_ref, 0, b_left))
        )
    ]
    for copy in copies:
        copy.start()
    sub = iota((8, LANES), 0)
    copies[0].wait()
    copies[1].wait()
    for r in range(N):
        w = DAMPING / (6.0 + s_right[r])
        right_ref[r] = jnp.where(sub < 4, pltpu.roll(w, 4, 0), w * b_right[r])
    copies[2].wait()
    copies[3].wait()
    for r in range(N):
        w = DAMPING / (6.0 + s_left[r])
        left_ref[r] = jnp.where(sub < 4, w, pltpu.roll(w * b_left[r], 4, 0))


def coefficients_kernel(b_ref, s_ref, mask_ref, id_ref, w_ref, wb_ref, info_ref):
    for r in range(N):
        w = DAMPING / (6.0 + s_ref[r])
        w_ref[r] = w
        wb_ref[r] = w * b_ref[r]
    sub = iota((8, LANES), 0)
    number = jnp.broadcast_to(id_ref[...].astype(F32), (8, LANES))
    mask = jnp.broadcast_to(mask_ref[...].astype(F32), (8, LANES))
    info_ref[...] = jnp.where(sub == 4, number, jnp.where(sub == 5, mask, 0.0))


def beside_of(left_msg, right_msg):
    sub = iota((8, LANES), 0)
    w = jnp.where(sub < 4, right_msg, pltpu.roll(left_msg, 4, 0))
    wb = jnp.where(sub < 4, pltpu.roll(right_msg, 4, 0), left_msg)
    return w, wb


def rows_kernel(w_ref, wb_ref, from_left_ref, from_right_ref, down_ref, up_ref):
    for target, start in ((up_ref, 0), (down_ref, N - HALO)):
        for k in range(HALO):
            r = start + k
            sides = beside_of(from_left_ref[r], from_right_ref[r])
            for a, ref in enumerate((w_ref, wb_ref)):
                target[a, k, 0:N] = ref[r]
                target[a, k, N:] = sides[a]


def first_inner_kernel(
    b_ref, s_ref, w_ref, wb_ref, from_left_ref, from_right_ref, v_ref, ww_ref, wwb_ref, saved_ref, partial_ref
):
    cross = lax.axis_index("cross")
    sub = iota((8, LANES), 0)
    in_left, in_right = (sub >= 4) & (cross > 0), (sub < 4) & (cross < lax.axis_size("cross") - 1)
    for r in range(N):
        w_side, wb_side = beside_of(from_left_ref[r], from_right_ref[r])
        for ref, own, side in ((ww_ref, w_ref[r], w_side), (wwb_ref, wb_ref[r], wb_side)):
            ref[r, 0:8] = jnp.where(in_left, side, 0.0)
            ref[r, 8 : 8 + N] = own
            ref[r, 8 + N :] = jnp.where(in_right, side, 0.0)
        v_ref[r] = wwb_ref[r]
    inner_sweeps(v_ref, ww_ref, wwb_ref, saved_ref, 3)
    for part in range(2):
        total = jnp.zeros((N, LANES), F32)
        for r in range(4 + 12 * part, 16 + 12 * part):
            total = total + fine_residual(v_ref[r - 1], v_ref[r], v_ref[r + 1], b_ref[r], s_ref[r])
        partial_ref[part] = total


def first_outer_kernel(
    b_ref, s_ref, v_ref, ww_ref, wwb_ref, saved_ref, partial_ref, below_ref, above_ref, info_ref,
    ends_ref, halo_ref, right_ref, left_ref, coarse_ref,
):
    span, cross = lax.axis_index("span"), lax.axis_index("cross")
    sub = iota((8, LANES), 0)
    in_left, in_right = (sub >= 4) & (cross > 0), (sub < 4) & (cross < lax.axis_size("cross") - 1)
    inside = (span > 0, span < lax.axis_size("span") - 1)
    for side, source in enumerate((above_ref, below_ref)):
        for a in range(2):
            for k in range(HALO):
                beside = source[a, k, N:]
                halo_ref[side, a, k, 0:8] = jnp.where(in_left & inside[side], beside, 0.0)
                halo_ref[side, a, k, 8 : 8 + N] = jnp.where(inside[side], source[a, k, 0:N], 0.0)
                halo_ref[side, a, k, 8 + N :] = jnp.where(in_right & inside[side], beside, 0.0)

    def coefficients(r):
        if 0 <= r < N:
            return ww_ref[r], wwb_ref[r]
        side, k = (0, r + HALO) if r < 0 else (1, r - N)
        return halo_ref[side, 0, k], halo_ref[side, 1, k]

    tile = info_ref[...]
    ends = outer_sweeps(
        [([coefficients(r)[1] for r in range(start, start + HALO + 2)], start) for start in (-HALO, N - 2)],
        3,
        coefficients,
        saved_ref,
    )
    for side, (rows, start) in enumerate(ends):
        total = partial_ref[side]
        for i in range(1, 5):
            r = start + i
            total = total + fine_residual(*rows[i - 1 : i + 2], b_ref[r], s_ref[r])
        for half in range(2):
            row = jnp.sum(total[half * CUBE : (half + 1) * CUBE], axis=0, keepdims=True)
            tile = jnp.where(sub == 2 * side + half, row, tile)
        for k in range(3):
            ends_ref[side, k] = rows[k + 1 + side]
    lane = iota((8, LANES), 1)
    cells = tile
    for step in (1, 2, 4, 8):
        cells = cells + jnp.where((lane & step) == 0, pltpu.roll(cells, LANES - step, 1), pltpu.roll(cells, step, 1))
    tile = jnp.where(sub < 4, cells / float(CUBE), tile)
    coarse_ref[...] = tile
    right_ref[16] = tile
    left_ref[16] = tile

    def pressure(r):
        return ends_ref.at[0, r] if r < 3 else (v_ref.at[r] if r < N - 3 else ends_ref.at[1, r - N + 3])

    for k in range(16):
        a, c = pressure(k), pressure(16 + k)
        right_ref[k] = jnp.where((sub >= 3) & (sub < 7), a[N : N + 8], pltpu.roll(c[N : N + 8], 4, 0))
        left_ref[k] = jnp.where((sub >= 1) & (sub < 5), a[8:16], pltpu.roll(c[8:16], 4, 0))


def correct_kernel(
    inner_ref, ends_ref, coarse_ref, far_right_ref, far_left_ref, from_left_ref, from_right_ref, v_ref, down_ref, up_ref, e_ref
):
    cross, n_cross = lax.axis_index("cross"), lax.axis_size("cross")
    has_left, has_right = cross > 0, cross < n_cross - 1
    sub = iota((8, LANES), 0)
    lane = iota((8, LANES), 1)
    even = (sub & 1) == 0

    def wide(row):
        return jnp.broadcast_to(row, (8, LANES))

    scale = [
        jnp.where((cross + d >= 0) & (cross + d < n_cross), F32(DAMPING / 6.0), F32(0.0)) for d in range(-2, 3)
    ]
    tiles = (far_left_ref, from_left_ref.at[16], coarse_ref, from_right_ref.at[16], far_right_ref)
    ids = [wide(t[4:5]) for t in tiles]
    masks = [wide(t[5:6]) for t in tiles]
    owner = jnp.where(sub < 2, ids[1], jnp.where(sub < 4, ids[2], ids[3]))
    strip = []
    for d in range(5):
        chosen = (ids[d] == owner) & (masks[d] > 0.5)
        for j in range(2):
            cells = jnp.where(even, wide(tiles[d][j : j + 1]), wide(tiles[d][2 + j : 3 + j]))
            strip.append(jnp.where(chosen, cells, 0.0))
    e = [scale[j // 2] * strip[j] for j in range(10)]
    for step in range(1, 4):
        new = list(e)
        for j in range(step, 10 - step):
            beside = e[j - 1] + e[j + 1]
            beside = beside + jnp.where(even, pltpu.roll(e[j], 7, 0), pltpu.roll(e[j], 1, 0))
            beside = beside + jnp.where(lane < CUBE, 0.0, pltpu.roll(e[j], CUBE, 1))
            beside = beside + jnp.where(lane >= LANES - CUBE, 0.0, pltpu.roll(e[j], LANES - CUBE, 1))
            new[j] = (1.0 - DAMPING) * e[j] + scale[j // 2] * (strip[j] + beside)
        e = new
    mask = jnp.where(
        sub < 2, jnp.where(has_left, masks[1], 0.0), jnp.where(sub < 4, masks[2], jnp.where(has_right, masks[3], 0.0))
    )
    for j in range(3, 7):
        e_ref[j - 3] = e[j] * mask

    in_left = (sub >= 3) & (sub < 7) & has_left
    in_right = (sub >= 1) & (sub < 5) & has_right
    for i in range(2):
        first, second = wide(e_ref[1, 2 + i : 3 + i]), wide(e_ref[2, 2 + i : 3 + i])
        own = jnp.concatenate([first, first, second, second], axis=0)
        beside = wide(e_ref[0, i : i + 1]), wide(e_ref[3, 4 + i : 5 + i])
        for k in range(CUBE):
            r = i * CUBE + k
            source = ends_ref.at[0, r] if r < 3 else (inner_ref.at[r] if r < N - 3 else ends_ref.at[1, r - N + 3])
            v_ref[r, 8 : 8 + N] = source[8 : 8 + N] + own
            left, right = from_left_ref[k], from_right_ref[k]
            if i == 1:
                left, right = pltpu.roll(left, 4, 0), pltpu.roll(right, 4, 0)
            left = jnp.where(in_left, left, jnp.where(sub == 7, source[0:8], 0.0))
            right = jnp.where(in_right, right, jnp.where(sub == 0, source[8 + N :], 0.0))
            v_ref[r, 0:8] = left + beside[0]
            v_ref[r, 8 + N :] = right + beside[1]
    for target, start in ((up_ref, 0), (down_ref, N - REACH)):
        for k in range(REACH):
            target[k, 0:N] = v_ref[start + k, 8 : 8 + N]
            target[k, N:] = jnp.where(sub < 4, v_ref[start + k, 8 + N :], v_ref[start + k, 0:8])


def second_inner_kernel(
    b_ref, s_ref, v_in_ref, ww_ref, wwb_ref, saved_ref, pressure_hbm, residual_hbm, v_ref, residual_ref, sems
):
    for r in range(N):
        v_ref[r] = v_in_ref[r]
    inner_sweeps(v_ref, ww_ref, wwb_ref, saved_ref, 4)
    low, high = 4, N - 4
    first = pltpu.make_async_copy(
        v_ref.at[pl.ds(low, high - low), pl.ds(8, N), :], pressure_hbm.at[pl.ds(low, high - low)], sems.at[0]
    )
    first.start()
    low = 5
    copies = [first]
    for place, count in ((5, 14), (19, 8)):
        for r in range(place, place + count):
            residual_ref[r - low] = fine_residual(v_ref[r - 1], v_ref[r], v_ref[r + 1], b_ref[r], s_ref[r])
        copies.append(
            pltpu.make_async_copy(
                residual_ref.at[pl.ds(place - low, count)], residual_hbm.at[pl.ds(place, count)], sems.at[len(copies)]
            )
        )
        copies[-1].start()
    for copy in copies:
        copy.wait()


def second_outer_kernel(
    b_ref, s_ref, v_ref, ww_ref, wwb_ref, halo_ref, saved_ref, below_ref, above_ref, pressure_in, residual_in,
    pressure_hbm, residual_hbm, pressure_ref, residual_ref, sems,
):
    span = lax.axis_index("span")
    inside = (span > 0, span < lax.axis_size("span") - 1)
    sub = iota((8, LANES), 0)

    def coefficients(r):
        if 0 <= r < N:
            return ww_ref[r], wwb_ref[r]
        side, k = (0, r + HALO) if r < 0 else (1, r - N)
        return halo_ref[side, 0, k], halo_ref[side, 1, k]

    copies, ends = [], []
    for side, source in enumerate((above_ref, below_ref)):
        outside = []
        for k in range(REACH):
            beside = source[k, N:]
            left = jnp.where((sub >= 4) & inside[side], beside, 0.0)
            right = jnp.where((sub < 4) & inside[side], beside, 0.0)
            outside.append(jnp.concatenate([left, jnp.where(inside[side], source[k, 0:N], 0.0), right], axis=0))
        ends.append((outside + [v_ref[0], v_ref[1]], -REACH) if side == 0 else ([v_ref[N - 2], v_ref[N - 1]] + outside, N - 2))
    ends = outer_sweeps(ends, 4, coefficients, saved_ref)
    def send(ref, hbm, count):
        for side in range(2):
            place = pl.ds(0 if side == 0 else N - count, count)
            copies.append(pltpu.make_async_copy(ref.at[side], hbm.at[place], sems.at[len(copies)]))
            copies[-1].start()

    for side, (rows, start) in enumerate(ends):
        for k in range(4):
            pressure_ref[side, k] = rows[k + 1 + side][8 : 8 + N]
    send(pressure_ref, pressure_hbm, 4)
    for side, (rows, start) in enumerate(ends):
        for i in range(1, 6):
            r = start + i
            residual_ref[side, i - 1] = fine_residual(*rows[i - 1 : i + 2], b_ref[r], s_ref[r])
    send(residual_ref, residual_hbm, 5)
    for copy in copies:
        copy.wait()


VMEM = pl.BlockSpec(memory_space=pltpu.VMEM)
HBM = pl.BlockSpec(memory_space=pltpu.HBM)


def call(kernel, outs, args, scratch=(), ins=None, out_specs=None, ops=0, room=32, aliases=None):
    size = 4 * sum(math.prod(s) for s in outs)
    return pl.pallas_call(
        kernel,
        out_shape=[jax.ShapeDtypeStruct(s, F32) for s in outs],
        in_specs=ins or [VMEM] * len(args),
        out_specs=out_specs or [VMEM] * len(outs),
        scratch_shapes=[pltpu.VMEM(s, F32) if isinstance(s, tuple) else s for s in scratch],
        input_output_aliases=aliases or {},
        compiler_params=pltpu.CompilerParams(vmem_limit_bytes=room * 1024 * 1024),
        cost_estimate=pl.CostEstimate(flops=ops, bytes_accessed=2 * size, transcendentals=0),
    )(*args)


def shifted(block, axis, step):
    count = lax.axis_size(axis)
    pairs = [(i, (i + step) % count) for i in range(count)]
    return lax.ppermute(block, axis, [p for p in pairs if axis == "span" or p[1] - p[0] == step])


def on_device(right_side, shift, tile_mask, owner_lists, owner_ids):
    block, wide, edge = (N, N, LANES), (N, WIDE, LANES), (N, 8, LANES)
    sems = pltpu.SemaphoreType.DMA
    right, left = call(
        edges_kernel, [edge, edge], [right_side, shift], scratch=[edge, edge, edge, edge, sems((4,))],
        ins=[HBM] * 2, room=60,
    )
    b, s, right, left = lax.optimization_barrier((right_side, shift, right, left))
    from_left = shifted(right, "cross", 1)
    from_right = shifted(left, "cross", -1)
    w, wb, info = call(
        coefficients_kernel, [block, block, (8, LANES)], [b, s, tile_mask, owner_ids], ops=2**20
    )
    rows = (2, HALO, N + 8, LANES)
    down, up = call(rows_kernel, [rows, rows], [w, wb, from_left, from_right])
    above = shifted(down, "span", 1)
    below = shifted(up, "span", -1)
    v, ww, wwb, saved, partial = call(
        first_inner_kernel,
        [wide, wide, wide, (2, 3, 2, WIDE, LANES), (2, N, LANES)],
        [b, s, w, wb, from_left, from_right],
        ops=2**23,
    )
    ends, halo, right, left, coarse = call(
        first_outer_kernel,
        [(2, 3, WIDE, LANES), (2, 2, HALO, WIDE, LANES), (17, 8, LANES), (17, 8, LANES), (8, LANES)],
        [b, s, v, ww, wwb, saved, partial, below, above, info],
    )
    far_left = shifted(coarse, "cross", 2)
    far_right = shifted(coarse, "cross", -2)
    from_left = shifted(right, "cross", 1)
    from_right = shifted(left, "cross", -1)
    rows = (REACH, N + 8, LANES)
    v, down, up = call(
        correct_kernel,
        [wide, rows, rows],
        [v, ends, coarse, far_right, far_left, from_left, from_right],
        scratch=[(4, 8, LANES)],
    )
    above = shifted(down, "span", 1)
    below = shifted(up, "span", -1)
    saved, pressure, residual = call(
        second_inner_kernel,
        [(2, 4, 2, WIDE, LANES), block, block],
        [b, s, v, ww, wwb],
        scratch=[wide, (N - 10, N, LANES), sems((3,))],
        out_specs=[VMEM, HBM, HBM],
        ops=2**23,
    )
    return tuple(
        call(
            second_outer_kernel,
            [block, block],
            [b, s, v, ww, wwb, halo, saved, below, above, pressure, residual],
            scratch=[(2, 4, N, LANES), (2, 5, N, LANES), sems((4,))],
            ins=[VMEM] * 9 + [HBM] * 2,
            out_specs=[HBM, HBM],
            aliases={9: 0, 10: 1},
        )
    )


def solution(mesh):
    return jax.shard_map(
        on_device,
        mesh=mesh,
        in_specs=(
            P("span", "cross", None),
            P("span", "cross", None),
            P("span", "cross"),
            P("span", "cross", None),
            P("span", "cross"),
        ),
        out_specs=(P("span", "cross", None), P("span", "cross", None)),
        check_vma=False,
    )
```

```python
import math

import jax
import jax.numpy as jnp
from jax import lax
from jax.experimental import pallas as pl
from jax.experimental.pallas import tpu as pltpu
from jax.sharding import PartitionSpec as P

DAMPING = 0.8
N = 32
LANES = 128
WIDE = N + 16
HALO = 4
REACH = 5
ROWS_W = N + 2 * HALO
ROWS_V = N + 2 * REACH
CUBE = 16
F32 = jnp.float32


def iota(shape, axis):
    return lax.broadcasted_iota(jnp.int32, shape, axis)


def neighbours(prev, cur, nxt):
    cells = cur.shape[0]
    lane = iota(cur.shape, 1)
    low = jnp.where(lane == 0, 0.0, pltpu.roll(cur, 1, 1))
    high = jnp.where(lane == LANES - 1, 0.0, pltpu.roll(cur, LANES - 1, 1))
    beside = pltpu.roll(cur, 1, 0) + pltpu.roll(cur, cells - 1, 0)
    return (prev + nxt) + beside + (low + high)


def swept(prev, cur, nxt, w, wb):
    return (1.0 - DAMPING) * cur + (wb + w * neighbours(prev, cur, nxt))


def inner_sweeps(v_ref, w_ref, wb_ref, saved_ref, count):
    def one(step, carry):
        prev, cur = v_ref[0], v_ref[1]
        for r in range(1, N - 1):
            nxt = v_ref[r + 1]
            v_ref[r] = swept(prev, cur, nxt, w_ref[r], wb_ref[r])
            prev, cur = cur, nxt
        for k in range(2):
            saved_ref[0, step, k] = v_ref[step + 1 + k]
            saved_ref[1, step, k] = v_ref[N - 3 - step + k]
        return carry

    lax.fori_loop(0, count, one, 0)


def outer_sweeps(ends, count, coefficients, saved_ref):
    for step in range(count):
        later = []
        for side, (rows, first) in enumerate(ends):
            new = [swept(*rows[i : i + 3], *coefficients(first + 1 + i)) for i in range(len(rows) - 2)]
            saved = [saved_ref[side, step, k] for k in range(2)]
            later.append((new + saved, first + 1) if side == 0 else (saved + new, first - 1))
        ends = later
    return ends


def fine_residual(prev, cur, nxt, b, s):
    own = slice(8, 8 + N)
    return b - ((6.0 + s) * cur[own] - neighbours(prev, cur, nxt)[own])


def edges_kernel(b_ref, s_ref, right_ref, left_ref, b_left, b_right, s_left, s_right, sems):
    copies = [
        pltpu.make_async_copy(source.at[:, pl.ds(start, 4), :], target.at[:, pl.ds(start % 8, 4), :], sems.at[n])
        for n, (source, start, target) in enumerate(
            ((s_ref, N - 4, s_right), (b_ref, N - 4, b_right), (s_ref, 0, s_left), (b_ref, 0, b_left))
        )
    ]
    for copy in copies:
        copy.start()
    sub = iota((8, LANES), 0)
    copies[0].wait()
    copies[1].wait()
    for r in range(N):
        w = DAMPING / (6.0 + s_right[r])
        right_ref[r] = jnp.where(sub < 4, pltpu.roll(w, 4, 0), w * b_right[r])
    copies[2].wait()
    copies[3].wait()
    for r in range(N):
        w = DAMPING / (6.0 + s_left[r])
        left_ref[r] = jnp.where(sub < 4, w, pltpu.roll(w * b_left[r], 4, 0))


def coefficients_kernel(b_ref, s_ref, mask_ref, id_ref, w_ref, wb_ref, info_ref):
    for r in range(N):
        w = DAMPING / (6.0 + s_ref[r])
        w_ref[r] = w
        wb_ref[r] = w * b_ref[r]
    sub = iota((8, LANES), 0)
    number = jnp.broadcast_to(id_ref[...].astype(F32), (8, LANES))
    mask = jnp.broadcast_to(mask_ref[...].astype(F32), (8, LANES))
    info_ref[...] = jnp.where(sub == 4, number, jnp.where(sub == 5, mask, 0.0))


def beside_of(left_msg, right_msg):
    sub = iota((8, LANES), 0)
    w = jnp.where(sub < 4, right_msg, pltpu.roll(left_msg, 4, 0))
    wb = jnp.where(sub < 4, pltpu.roll(right_msg, 4, 0), left_msg)
    return w, wb


def rows_kernel(w_ref, wb_ref, from_left_ref, from_right_ref, down_ref, up_ref):
    for target, start in ((up_ref, 0), (down_ref, N - HALO)):
        for k in range(HALO):
            r = start + k
            sides = beside_of(from_left_ref[r], from_right_ref[r])
            for a, ref in enumerate((w_ref, wb_ref)):
                target[a, k, 0:N] = ref[r]
                target[a, k, N:] = sides[a]


def first_inner_kernel(
    b_ref, s_ref, w_ref, wb_ref, from_left_ref, from_right_ref, v_ref, ww_ref, wwb_ref, saved_ref, partial_ref
):
    cross = lax.axis_index("cross")
    sub = iota((8, LANES), 0)
    in_left, in_right = (sub >= 4) & (cross > 0), (sub < 4) & (cross < lax.axis_size("cross") - 1)
    for r in range(N):
        w_side, wb_side = beside_of(from_left_ref[r], from_right_ref[r])
        for ref, own, side in ((ww_ref, w_ref[r], w_side), (wwb_ref, wb_ref[r], wb_side)):
            ref[r, 0:8] = jnp.where(in_left, side, 0.0)
            ref[r, 8 : 8 + N] = own
            ref[r, 8 + N :] = jnp.where(in_right, side, 0.0)
        v_ref[r] = wwb_ref[r]
    inner_sweeps(v_ref, ww_ref, wwb_ref, saved_ref, 3)
    for part in range(2):
        total = jnp.zeros((N, LANES), F32)
        for r in range(4 + 12 * part, 16 + 12 * part):
            total = total + fine_residual(v_ref[r - 1], v_ref[r], v_ref[r + 1], b_ref[r], s_ref[r])
        partial_ref[part] = total


def first_outer_kernel(
    b_ref, s_ref, v_ref, ww_ref, wwb_ref, saved_ref, partial_ref, below_ref, above_ref, info_ref,
    ends_ref, halo_ref, right_ref, left_ref, coarse_ref,
):
    span, cross = lax.axis_index("span"), lax.axis_index("cross")
    sub = iota((8, LANES), 0)
    in_left, in_right = (sub >= 4) & (cross > 0), (sub < 4) & (cross < lax.axis_size("cross") - 1)
    inside = (span > 0, span < lax.axis_size("span") - 1)
    for side, source in enumerate((above_ref, below_ref)):
        for a in range(2):
            for k in range(HALO):
                beside = source[a, k, N:]
                halo_ref[side, a, k, 0:8] = jnp.where(in_left & inside[side], beside, 0.0)
                halo_ref[side, a, k, 8 : 8 + N] = jnp.where(inside[side], source[a, k, 0:N], 0.0)
                halo_ref[side, a, k, 8 + N :] = jnp.where(in_right & inside[side], beside, 0.0)

    def coefficients(r):
        if 0 <= r < N:
            return ww_ref[r], wwb_ref[r]
        side, k = (0, r + HALO) if r < 0 else (1, r - N)
        return halo_ref[side, 0, k], halo_ref[side, 1, k]

    tile = info_ref[...]
    ends = outer_sweeps(
        [([coefficients(r)[1] for r in range(start, start + HALO + 2)], start) for start in (-HALO, N - 2)],
        3,
        coefficients,
        saved_ref,
    )
    for side, (rows, start) in enumerate(ends):
        total = partial_ref[side]
        for i in range(1, 5):
            r = start + i
            total = total + fine_residual(*rows[i - 1 : i + 2], b_ref[r], s_ref[r])
        for half in range(2):
            row = jnp.sum(total[half * CUBE : (half + 1) * CUBE], axis=0, keepdims=True)
            tile = jnp.where(sub == 2 * side + half, row, tile)
        for k in range(3):
            ends_ref[side, k] = rows[k + 1 + side]
    lane = iota((8, LANES), 1)
    cells = tile
    for step in (1, 2, 4, 8):
        cells = cells + jnp.where((lane & step) == 0, pltpu.roll(cells, LANES - step, 1), pltpu.roll(cells, step, 1))
    tile = jnp.where(sub < 4, cells / float(CUBE), tile)
    coarse_ref[...] = tile
    right_ref[16] = tile
    left_ref[16] = tile

    def pressure(r):
        return ends_ref.at[0, r] if r < 3 else (v_ref.at[r] if r < N - 3 else ends_ref.at[1, r - N + 3])

    for k in range(16):
        a, c = pressure(k), pressure(16 + k)
        right_ref[k] = jnp.where((sub >= 3) & (sub < 7), a[N : N + 8], pltpu.roll(c[N : N + 8], 4, 0))
        left_ref[k] = jnp.where((sub >= 1) & (sub < 5), a[8:16], pltpu.roll(c[8:16], 4, 0))


def correct_kernel(
    inner_ref, ends_ref, coarse_ref, far_right_ref, far_left_ref, from_left_ref, from_right_ref, v_ref, down_ref, up_ref, e_ref
):
    cross, n_cross = lax.axis_index("cross"), lax.axis_size("cross")
    has_left, has_right = cross > 0, cross < n_cross - 1
    sub = iota((8, LANES), 0)
    lane = iota((8, LANES), 1)
    even = (sub & 1) == 0

    def wide(row):
        return jnp.broadcast_to(row, (8, LANES))

    scale = [
        jnp.where((cross + d >= 0) & (cross + d < n_cross), F32(DAMPING / 6.0), F32(0.0)) for d in range(-2, 3)
    ]
    tiles = (far_left_ref, from_left_ref.at[16], coarse_ref, from_right_ref.at[16], far_right_ref)
    ids = [wide(t[4:5]) for t in tiles]
    masks = [wide(t[5:6]) for t in tiles]
    owner = jnp.where(sub < 2, ids[1], jnp.where(sub < 4, ids[2], ids[3]))
    strip = []
    for d in range(5):
        chosen = (ids[d] == owner) & (masks[d] > 0.5)
        for j in range(2):
            cells = jnp.where(even, wide(tiles[d][j : j + 1]), wide(tiles[d][2 + j : 3 + j]))
            strip.append(jnp.where(chosen, cells, 0.0))
    e = [scale[j // 2] * strip[j] for j in range(10)]
    for step in range(1, 4):
        new = list(e)
        for j in range(step, 10 - step):
            beside = e[j - 1] + e[j + 1]
            beside = beside + jnp.where(even, pltpu.roll(e[j], 7, 0), pltpu.roll(e[j], 1, 0))
            beside = beside + jnp.where(lane < CUBE, 0.0, pltpu.roll(e[j], CUBE, 1))
            beside = beside + jnp.where(lane >= LANES - CUBE, 0.0, pltpu.roll(e[j], LANES - CUBE, 1))
            new[j] = (1.0 - DAMPING) * e[j] + scale[j // 2] * (strip[j] + beside)
        e = new
    mask = jnp.where(
        sub < 2, jnp.where(has_left, masks[1], 0.0), jnp.where(sub < 4, masks[2], jnp.where(has_right, masks[3], 0.0))
    )
    for j in range(3, 7):
        e_ref[j - 3] = e[j] * mask

    in_left = (sub >= 3) & (sub < 7) & has_left
    in_right = (sub >= 1) & (sub < 5) & has_right
    for i in range(2):
        first, second = wide(e_ref[1, 2 + i : 3 + i]), wide(e_ref[2, 2 + i : 3 + i])
        own = jnp.concatenate([first, first, second, second], axis=0)
        beside = wide(e_ref[0, i : i + 1]), wide(e_ref[3, 4 + i : 5 + i])
        for k in range(CUBE):
            r = i * CUBE + k
            source = ends_ref.at[0, r] if r < 3 else (inner_ref.at[r] if r < N - 3 else ends_ref.at[1, r - N + 3])
            v_ref[r, 8 : 8 + N] = source[8 : 8 + N] + own
            left, right = from_left_ref[k], from_right_ref[k]
            if i == 1:
                left, right = pltpu.roll(left, 4, 0), pltpu.roll(right, 4, 0)
            left = jnp.where(in_left, left, jnp.where(sub == 7, source[0:8], 0.0))
            right = jnp.where(in_right, right, jnp.where(sub == 0, source[8 + N :], 0.0))
            v_ref[r, 0:8] = left + beside[0]
            v_ref[r, 8 + N :] = right + beside[1]
    for target, start in ((up_ref, 0), (down_ref, N - REACH)):
        for k in range(REACH):
            target[k, 0:N] = v_ref[start + k, 8 : 8 + N]
            target[k, N:] = jnp.where(sub < 4, v_ref[start + k, 8 + N :], v_ref[start + k, 0:8])


def second_inner_kernel(
    b_ref, s_ref, v_in_ref, ww_ref, wwb_ref, saved_ref, pressure_hbm, residual_hbm, v_ref, residual_ref, sems
):
    for r in range(N):
        v_ref[r] = v_in_ref[r]
    inner_sweeps(v_ref, ww_ref, wwb_ref, saved_ref, 4)
    low, high = 4, N - 4
    first = pltpu.make_async_copy(
        v_ref.at[pl.ds(low, high - low), pl.ds(8, N), :], pressure_hbm.at[pl.ds(low, high - low)], sems.at[0]
    )
    first.start()
    low = 5
    copies = [first]
    for place, count in ((5, 17), (22, 5)):
        for r in range(place, place + count):
            residual_ref[r - low] = fine_residual(v_ref[r - 1], v_ref[r], v_ref[r + 1], b_ref[r], s_ref[r])
        copies.append(
            pltpu.make_async_copy(
                residual_ref.at[pl.ds(place - low, count)], residual_hbm.at[pl.ds(place, count)], sems.at[len(copies)]
            )
        )
        copies[-1].start()
    for copy in copies:
        copy.wait()


def second_outer_kernel(
    b_ref, s_ref, v_ref, ww_ref, wwb_ref, halo_ref, saved_ref, below_ref, above_ref, pressure_in, residual_in,
    pressure_hbm, residual_hbm, pressure_ref, residual_ref, sems,
):
    span = lax.axis_index("span")
    inside = (span > 0, span < lax.axis_size("span") - 1)
    sub = iota((8, LANES), 0)

    def coefficients(r):
        if 0 <= r < N:
            return ww_ref[r], wwb_ref[r]
        side, k = (0, r + HALO) if r < 0 else (1, r - N)
        return halo_ref[side, 0, k], halo_ref[side, 1, k]

    copies, ends = [], []
    for side, source in enumerate((above_ref, below_ref)):
        outside = []
        for k in range(REACH):
            beside = source[k, N:]
            left = jnp.where((sub >= 4) & inside[side], beside, 0.0)
            right = jnp.where((sub < 4) & inside[side], beside, 0.0)
            outside.append(jnp.concatenate([left, jnp.where(inside[side], source[k, 0:N], 0.0), right], axis=0))
        ends.append((outside + [v_ref[0], v_ref[1]], -REACH) if side == 0 else ([v_ref[N - 2], v_ref[N - 1]] + outside, N - 2))
    ends = outer_sweeps(ends, 4, coefficients, saved_ref)
    def send(ref, hbm, count):
        for side in range(2):
            place = pl.ds(0 if side == 0 else N - count, count)
            copies.append(pltpu.make_async_copy(ref.at[side], hbm.at[place], sems.at[len(copies)]))
            copies[-1].start()

    for side, (rows, start) in enumerate(ends):
        for k in range(4):
            pressure_ref[side, k] = rows[k + 1 + side][8 : 8 + N]
    send(pressure_ref, pressure_hbm, 4)
    for side, (rows, start) in enumerate(ends):
        for i in range(1, 6):
            r = start + i
            residual_ref[side, i - 1] = fine_residual(*rows[i - 1 : i + 2], b_ref[r], s_ref[r])
    send(residual_ref, residual_hbm, 5)
    for copy in copies:
        copy.wait()


VMEM = pl.BlockSpec(memory_space=pltpu.VMEM)
HBM = pl.BlockSpec(memory_space=pltpu.HBM)


def call(kernel, outs, args, scratch=(), ins=None, out_specs=None, ops=0, room=32, aliases=None):
    size = 4 * sum(math.prod(s) for s in outs)
    return pl.pallas_call(
        kernel,
        out_shape=[jax.ShapeDtypeStruct(s, F32) for s in outs],
        in_specs=ins or [VMEM] * len(args),
        out_specs=out_specs or [VMEM] * len(outs),
        scratch_shapes=[pltpu.VMEM(s, F32) if isinstance(s, tuple) else s for s in scratch],
        input_output_aliases=aliases or {},
        compiler_params=pltpu.CompilerParams(vmem_limit_bytes=room * 1024 * 1024),
        cost_estimate=pl.CostEstimate(flops=ops, bytes_accessed=2 * size, transcendentals=0),
    )(*args)


def shifted(block, axis, step):
    count = lax.axis_size(axis)
    pairs = [(i, (i + step) % count) for i in range(count)]
    return lax.ppermute(block, axis, [p for p in pairs if axis == "span" or p[1] - p[0] == step])


def on_device(right_side, shift, tile_mask, owner_lists, owner_ids):
    block, wide, edge = (N, N, LANES), (N, WIDE, LANES), (N, 8, LANES)
    sems = pltpu.SemaphoreType.DMA
    right, left = call(
        edges_kernel, [edge, edge], [right_side, shift], scratch=[edge, edge, edge, edge, sems((4,))],
        ins=[HBM] * 2, room=60,
    )
    b, s, right, left = lax.optimization_barrier((right_side, shift, right, left))
    from_left = shifted(right, "cross", 1)
    from_right = shifted(left, "cross", -1)
    w, wb, info = call(
        coefficients_kernel, [block, block, (8, LANES)], [b, s, tile_mask, owner_ids], ops=2**20
    )
    rows = (2, HALO, N + 8, LANES)
    down, up = call(rows_kernel, [rows, rows], [w, wb, from_left, from_right])
    above = shifted(down, "span", 1)
    below = shifted(up, "span", -1)
    v, ww, wwb, saved, partial = call(
        first_inner_kernel,
        [wide, wide, wide, (2, 3, 2, WIDE, LANES), (2, N, LANES)],
        [b, s, w, wb, from_left, from_right],
        ops=2**23,
    )
    ends, halo, right, left, coarse = call(
        first_outer_kernel,
        [(2, 3, WIDE, LANES), (2, 2, HALO, WIDE, LANES), (17, 8, LANES), (17, 8, LANES), (8, LANES)],
        [b, s, v, ww, wwb, saved, partial, below, above, info],
    )
    far_left = shifted(coarse, "cross", 2)
    far_right = shifted(coarse, "cross", -2)
    from_left = shifted(right, "cross", 1)
    from_right = shifted(left, "cross", -1)
    rows = (REACH, N + 8, LANES)
    v, down, up = call(
        correct_kernel,
        [wide, rows, rows],
        [v, ends, coarse, far_right, far_left, from_left, from_right],
        scratch=[(4, 8, LANES)],
    )
    above = shifted(down, "span", 1)
    below = shifted(up, "span", -1)
    saved, pressure, residual = call(
        second_inner_kernel,
        [(2, 4, 2, WIDE, LANES), block, block],
        [b, s, v, ww, wwb],
        scratch=[wide, (N - 10, N, LANES), sems((3,))],
        out_specs=[VMEM, HBM, HBM],
        ops=2**23,
    )
    return tuple(
        call(
            second_outer_kernel,
            [block, block],
            [b, s, v, ww, wwb, halo, saved, below, above, pressure, residual],
            scratch=[(2, 4, N, LANES), (2, 5, N, LANES), sems((4,))],
            ins=[VMEM] * 9 + [HBM] * 2,
            out_specs=[HBM, HBM],
            aliases={9: 0, 10: 1},
        )
    )


def solution(mesh):
    return jax.shard_map(
        on_device,
        mesh=mesh,
        in_specs=(
            P("span", "cross", None),
            P("span", "cross", None),
            P("span", "cross"),
            P("span", "cross", None),
            P("span", "cross"),
        ),
        out_specs=(P("span", "cross", None), P("span", "cross", None)),
        check_vma=False,
    )
```
